32 devices in a mesh: stream: 4 (over x, core), cross: 8 (over z, y).
Axes of the slice: x: 2, y: 2, z: 4, core: 2. Of those that a mesh axis runs over, the one named last changes fastest.
Arguments:
- residual: bfloat16 [16, 64, 64, 128], P('stream', 'cross'), may hold values from -6 to 6
- approx_inverse: bfloat16 [4, 768, 64, 256], P('stream', 'cross'), may hold values from -0.375 to 0.375
- pattern: int32 [4, 768, 4], P('stream', 'cross'), may hold values from 0 to 95
- live_blocks: int32 [4, 8], P('stream', 'cross'), may hold values from 1 to 32, as said below
- block_aggregate: int32 [16, 64], P('stream', 'cross'), may hold values from 0 to 31
- coarse_inverse: float32 [128, 256], P('stream', 'cross'), may hold values from -0.12 to 0.12
Outputs:
- correction: float32 [16, 64, 64, 128], P('stream', 'cross')
The draws below stay inside these ranges and needn't reach their ends.
Inputs may be any that keep to these rules, and one draw needn't show every extreme that they name: `pattern`: block numbers of the extended grid, numbered row by row. `live_blocks`: some subdomain is full in every draw.
All inputs are finite; a program needn't handle non-finite values.
Results may differ from the reference program's by a relative error of at most 0.0065.
Values may be sent and summed in bfloat16 or wider, within the bound.
A program may use at most 64 MiB of HBM per device.

```python
import jax
import jax.numpy as jnp
from jax import lax

BLOCK = 64
CELLS = 16
K = 4
GS = 4
GC = 8
NRHS = 128
AGG_DEV = 8
NE = 96
NAG = 32
NSB = 16
NCB = 64
N_STREAM = 4
N_CROSS = 8


def draw_live_blocks(key, part):
    first, second = jax.random.split(jax.random.fold_in(key, 17))
    counts = jax.random.randint(first, (N_STREAM * N_CROSS,), 1, GS * GC + 1)
    chosen = jax.random.randint(second, (), 0, N_STREAM * N_CROSS)
    filled = jnp.where(jnp.arange(N_STREAM * N_CROSS) == chosen, GS * GC, counts)
    return filled.reshape(N_STREAM, N_CROSS).astype(jnp.int32)


def set_ends(array, key, smallest, top_value):
    index_at = [jax.random.randint(jax.random.fold_in(key, axis), (), 0, length) for axis, length in enumerate(array.shape)]
    widest = array.shape.index(max(array.shape))
    next_to = index_at[:widest] + [(index_at[widest] + 1) % array.shape[widest]] + index_at[widest + 1:]
    return array.at[tuple(index_at)].set(smallest).at[tuple(next_to)].set(top_value)


def levels(rng, dims, cuts, least, high):
    loudness = 1.0
    for dim, blocks in cuts:
        steps = jax.random.uniform(jax.random.fold_in(jax.random.fold_in(rng, 6), dim), (blocks,), jnp.float32, least / len(cuts), high / len(cuts))
        loudness = loudness * jnp.repeat(jnp.exp(steps), dims[dim] // blocks).reshape((-1,) + (1,) * (len(dims) - 1 - dim))
    return loudness


def noise(rng, extent, scale, bound, pieces=(), kind=jnp.bfloat16):
    factor_of = levels(rng, extent, pieces, -0.22, 0.18) if pieces else 1.0
    entries = jax.random.normal(rng, extent, jnp.float32) * scale * factor_of
    return jnp.minimum(jnp.maximum(entries, -bound), bound).astype(kind)


def setup_inputs(seed: int = 0) -> dict:
    keys = jax.random.split(jax.random.key(seed), 7)
    residual = noise(keys[0], (NSB, NCB, BLOCK, NRHS), 1.0, 6.0, ((0, 4), (1, 8)))
    approx_inverse = noise(keys[1], (N_STREAM, N_CROSS * NE, BLOCK, K * BLOCK), (K * BLOCK) ** -0.5, 0.375, ((0, 4), (1, 8)))
    pattern = set_ends(jax.random.randint(keys[2], (N_STREAM, N_CROSS * NE, K), 0, NE), jax.random.fold_in(keys[2], 1), 0, NE - 1).astype(jnp.int32)
    live_blocks = draw_live_blocks(jax.random.fold_in(keys[6], 71), 0)
    block_aggregate = set_ends(jax.random.randint(keys[4], (NSB, NCB), 0, NAG), jax.random.fold_in(keys[4], 1), 0, NAG - 1).astype(jnp.int32)
    coarse_inverse = noise(keys[5], (N_STREAM * AGG_DEV * 4, N_CROSS * AGG_DEV * 4), 0.02, 0.12, ((0, 4), (1, 8)), jnp.float32)
    return {"residual": residual, "approx_inverse": approx_inverse, "pattern": pattern, "live_blocks": live_blocks, "block_aggregate": block_aggregate, "coarse_inverse": coarse_inverse}


def reference(residual, approx_inverse, pattern, live_blocks, block_aggregate, coarse_inverse):
    nsb = residual.shape[0]
    ncb = residual.shape[1]
    row_local = jnp.arange(nsb) % GS
    col_local = jnp.arange(ncb) % GC
    local = row_local[:, None] * GC + col_local[None, :]
    counted = jnp.repeat(jnp.repeat(live_blocks, GS, axis=0), GC, axis=1)
    live = local < counted
    masked = jnp.where(live[:, :, None, None], residual, jnp.zeros((), jnp.bfloat16))
    padded = jnp.pad(masked, ((2, 2), (2, 2), (0, 0), (0, 0)))
    zero = jnp.zeros((), jnp.int32)

    def visit(index, total):
        index = jnp.asarray(index).astype(jnp.int32)
        sidx = index // N_CROSS
        cidx = index % N_CROSS
        start = (sidx * GS, cidx * GC, zero, zero)
        extended = lax.dynamic_slice(padded, start, (GS + 4, GC + 4, BLOCK, NRHS)).reshape(NE, BLOCK, NRHS)
        blocks = lax.dynamic_slice(approx_inverse, (sidx, cidx * NE, zero, zero), (1, NE, BLOCK, K * BLOCK))[0]
        links = lax.dynamic_slice(pattern, (sidx, cidx * NE, zero), (1, NE, K))[0]
        picked = extended[links].reshape(NE, K * BLOCK, NRHS)
        local_fix = jnp.einsum("nac,ncr->nar", blocks.astype(jnp.float32), picked.astype(jnp.float32),
                               precision=lax.Precision.HIGHEST).reshape(GS + 4, GC + 4, BLOCK, NRHS)
        rounded = lax.optimization_barrier(local_fix.astype(jnp.bfloat16)).astype(jnp.float32)
        here = lax.dynamic_slice(total, start, (GS + 4, GC + 4, BLOCK, NRHS))
        return lax.dynamic_update_slice(total, here + rounded, start)

    total = lax.fori_loop(0, N_STREAM * N_CROSS, visit, jnp.zeros(padded.shape, jnp.float32))
    fine = total[2:-2, 2:-2]
    per_block = masked.astype(jnp.float32).reshape(nsb, ncb, 4, CELLS, NRHS).sum(axis=3).reshape(nsb, ncb, 4 * NRHS)

    def group(cidx):
        cidx = cidx.astype(jnp.int32)
        sums = lax.dynamic_slice(per_block, (zero, cidx * GC, zero), (nsb, GC, 4 * NRHS)).reshape(nsb * GC, 4 * NRHS)
        labels = lax.dynamic_slice(block_aggregate, (zero, cidx * GC), (nsb, GC)).reshape(-1)
        onehot = (labels[:, None] == jnp.arange(NAG, dtype=jnp.int32)[None, :]).astype(jnp.float32)
        coarse_residual = jnp.dot(onehot.T, sums, precision=lax.Precision.HIGHEST)
        inverse = lax.dynamic_slice(coarse_inverse, (zero, cidx * AGG_DEV * 4), (N_STREAM * AGG_DEV * 4, AGG_DEV * 4))
        inverse = inverse.reshape(N_STREAM, AGG_DEV * 4, AGG_DEV * 4)
        coarse = jnp.einsum("sij,sjr->sir", inverse, coarse_residual.reshape(N_STREAM, AGG_DEV * 4, NRHS),
                            precision=lax.Precision.HIGHEST).reshape(NAG, 4 * NRHS)
        return jnp.dot(onehot, coarse, precision=lax.Precision.HIGHEST).reshape(nsb, GC, 4 * NRHS)

    prolonged = lax.map(group, jnp.arange(N_CROSS, dtype=jnp.int32))
    prolonged = jnp.transpose(prolonged, (1, 0, 2, 3)).reshape(nsb, ncb, 4, 1, NRHS)
    spread = jnp.broadcast_to(prolonged, (nsb, ncb, 4, CELLS, NRHS)).reshape(nsb, ncb, BLOCK, NRHS)
    return jnp.where(live[:, :, None, None], fine + spread, jnp.zeros((), jnp.float32))
```

```python
import functools

import jax
import jax.numpy as jnp
from jax import lax
from jax.experimental import pallas as pl
from jax.experimental.pallas import tpu as pltpu
from jax.sharding import PartitionSpec as P

W = 2


def kernel(
    ns, nc, R, C,
    residual, inverse, pattern, live_ref, aggregate, coarse_inv,
    out,
    res, a_mat, ext4, fix4, rs, rc, msum, pb, partial, part_in, coarse_all,
    in_sem, h_send, h_recv, q_send, q_recv, p_send, p_recv, g_send, g_recv,
    b_send, b_recv, d_send, d_recv,
):
    s = lax.axis_index("stream")
    c = lax.axis_index("cross")
    width, sides = res.shape[2], res.shape[3]
    CE = C + 2 * W
    RE = R + 2 * W
    owned = coarse_inv.shape[0] // 4
    bf16, f32 = jnp.bfloat16, jnp.float32

    s_has = (s > 0, s < ns - 1)
    c_has = (c > 0, c < nc - 1)
    s_to = (jnp.maximum(s - 1, 0), jnp.minimum(s + 1, ns - 1))
    c_to = (jnp.maximum(c - 1, 0), jnp.minimum(c + 1, nc - 1))

    load_res = pltpu.make_async_copy(residual, res, in_sem.at[0])
    load_a = pltpu.make_async_copy(inverse.at[0], a_mat, in_sem.at[1])
    load_res.start()
    load_a.start()

    barrier = pltpu.get_barrier_semaphore()
    for k in range(1, ns):
        pl.semaphore_signal(barrier, inc=1, device_id={"stream": lax.rem(s + k, ns)},
                            device_id_type=pl.DeviceIdType.MESH)
    for e in range(2):
        @pl.when(c_has[e])
        def _():
            pl.semaphore_signal(barrier, inc=1, device_id={"cross": c_to[e]},
                                device_id_type=pl.DeviceIdType.MESH)

    def zero(ref, rows, cols):
        ref[rows[0]:rows[1], cols[0]:cols[1]] = jnp.zeros(
            (rows[1] - rows[0], cols[1] - cols[0], width, sides), bf16)

    @pl.when(s == 0)
    def _():
        zero(ext4, (0, W), (0, CE))
        zero(rs, (0, W), (0, CE))

    @pl.when(s == ns - 1)
    def _():
        zero(ext4, (R + W, RE), (0, CE))
        zero(rs, (W, 2 * W), (0, CE))

    @pl.when(c == 0)
    def _():
        zero(ext4, (0, RE), (0, W))
        zero(rc, (0, R), (0, W))

    @pl.when(c == nc - 1)
    def _():
        zero(ext4, (0, RE), (C + W, CE))
        zero(rc, (0, R), (W, 2 * W))

    live = live_ref[0, 0]
    load_res.wait()

    def mask_row(i, carry):
        for j in range(C):
            block = res[i, j]
            keep = jnp.full(block.shape, i * C + j, jnp.int32) < live
            ext4[i + W, j + W] = jnp.where(keep, block.astype(f32), 0.0).astype(bf16)
        return carry

    lax.fori_loop(0, R, mask_row, 0, unroll=True)

    own_rows = (pl.ds(W, W), pl.ds(R, W))
    halo_rows = (pl.ds(R + W, W), pl.ds(0, W))
    own_cols = (pl.ds(W, W), pl.ds(C, W))
    halo_cols = (pl.ds(C + W, W), pl.ds(0, W))
    side_cols = (pl.ds(0, W), pl.ds(C + W, W))
    mid_rows, mid_cols = pl.ds(W, R), pl.ds(W, C)

    def remote(src, dst, send, recv, to):
        return pltpu.make_async_remote_copy(
            src_ref=src, dst_ref=dst, send_sem=send, recv_sem=recv,
            device_id=to, device_id_type=pl.DeviceIdType.MESH)

    def cross1(e):
        return remote(ext4.at[mid_rows, own_cols[e]], ext4.at[mid_rows, halo_cols[e]],
                      h_send.at[e], h_recv.at[e], {"cross": c_to[e]})

    def stream1(d):
        return remote(ext4.at[own_rows[d], mid_cols], ext4.at[halo_rows[d], mid_cols],
                      h_send.at[2 + d], h_recv.at[2 + d], {"stream": s_to[d]})

    def corner1(d, e):
        return remote(ext4.at[own_rows[d], side_cols[e]], ext4.at[halo_rows[d], side_cols[e]],
                      q_send.at[2 * d + e], q_recv.at[2 * d + e], {"stream": s_to[d]})

    far_rows = (pl.ds(0, W), pl.ds(R + W, W))
    land_rows = (pl.ds(W, W), pl.ds(0, W))

    def corner2(d, e):
        return remote(fix4.at[far_rows[d], side_cols[e]], rs.at[land_rows[d], side_cols[e]],
                      b_send.at[2 * d + e], b_recv.at[2 * d + e], {"stream": s_to[d]})

    def stream2(d):
        return remote(fix4.at[far_rows[d], mid_cols], rs.at[land_rows[d], mid_cols],
                      d_send.at[2 + d], d_recv.at[2 + d], {"stream": s_to[d]})

    def cross2(e):
        return remote(msum.at[:, pl.ds(W * e, W)], rc.at[:, pl.ds(W * (1 - e), W)],
                      d_send.at[e], d_recv.at[e], {"cross": c_to[e]})

    def when(cond, run):
        pl.when(cond)(run)

    pl.semaphore_wait(barrier, ns - 1 + c_has[0].astype(jnp.int32) + c_has[1].astype(jnp.int32))

    for e in range(2):
        when(c_has[e], lambda: cross1(e).start())
    for d in range(2):
        when(s_has[d], lambda: stream1(d).start())

    def sums(m, carry):
        i = m // (C // 2)
        j = (m % (C // 2)) * 2
        rows = []
        for t in range(2):
            block = ext4[i + W, j + W + t].astype(f32)
            rows.append(block.reshape(4, width // 4, sides).sum(axis=1))
        pb[pl.ds(pl.multiple_of(m * 8, 8), 8), :] = jnp.concatenate(rows, axis=0)
        return carry

    lax.fori_loop(0, R * C // 2, sums, 0, unroll=True)
    n_own = R * C
    lane = lax.broadcasted_iota(jnp.int32, (8, 4 * n_own), 1)
    key = jnp.zeros((8, 4 * n_own), jnp.int32)
    for i in range(R):
        for j in range(C):
            key = jnp.where(lane // 4 == i * C + j, aggregate[i, j], key)
    key = (key * 4 + lane % 4)[0:1]
    for o in range(ns):
        row = lax.broadcasted_iota(jnp.int32, (4 * owned, 4 * n_own), 0) + o * 4 * owned
        chosen = (row == jnp.broadcast_to(key, row.shape)).astype(f32)
        partial[o] = jnp.dot(chosen, pb[...], precision=lax.Precision.HIGHEST,
                             preferred_element_type=f32)

    def give(k):
        to = lax.rem(s + k, ns)
        return remote(partial.at[to], part_in.at[k - 1], p_send.at[k - 1], p_recv.at[k - 1],
                      {"stream": to})

    def share(k, mine):
        part = coarse_all.at[pl.ds(mine * owned, owned)]
        return remote(part, part, g_send.at[k - 1], g_recv.at[k - 1],
                      {"stream": lax.rem(s + k, ns)})

    for k in range(1, ns):
        give(k).start()

    for e in range(2):
        when(c_has[1 - e], lambda: cross1(e).wait_recv())
    for d in range(2):
        for e in range(2):
            when(s_has[d] & c_has[e], lambda: corner1(d, e).start())

    total = partial[s]
    for k in range(1, ns):
        give(k).wait_recv()
        total = total + part_in[k - 1]
    coarse = jnp.dot(coarse_inv[...], total, precision=lax.Precision.HIGHEST,
                     preferred_element_type=f32)
    for a in range(owned):
        coarse_all[s * owned + a] = coarse[4 * a:4 * a + 4]
    for k in range(1, ns):
        share(k, s).start()

    load_a.wait()
    for d in range(2):
        when(s_has[1 - d], lambda: stream1(d).wait_recv())
    for d in range(2):
        for e in range(2):
            when(s_has[1 - d] & c_has[e], lambda: corner1(d, e).wait_recv())

    ext = ext4.reshape(RE * CE, width, sides)

    def fix_of(i, j):
        n = i * CE + j
        picked = jnp.concatenate(
            [ext[pattern[0, n, k]] for k in range(a_mat.shape[2] // width)], axis=0)
        return jnp.dot(a_mat[n], picked, preferred_element_type=f32)

    edge = tuple(range(W)) + tuple(range(C + W, CE))

    def sweep(row_of, cols):
        def one(t, carry):
            i = row_of(t)
            for j in cols:
                fix4[i, j] = fix_of(i, j).astype(bf16)
            return carry

        lax.fori_loop(0, 2 * W, one, 0, unroll=True)

    outer = lambda t: t + (t // W) * R
    inner = lambda t: t + W
    sweep(outer, edge)
    for d in range(2):
        for e in range(2):
            when(s_has[d] & c_has[e], lambda: corner2(d, e).start())
    sweep(inner, edge)
    sweep(outer, range(W, C + W))
    for d in range(2):
        when(s_has[d], lambda: stream2(d).start())

    for e in range(2):
        @pl.when(c_has[e])
        def _():
            for d in range(2):
                when(s_has[1 - d], lambda: corner2(d, e).wait_recv())
            for i in range(R):
                for j in range(W):
                    col = e * (C + W) + j
                    msum[i, e * W + j] = (
                        fix4[i + W, col].astype(f32) + rs[i, col].astype(f32)).astype(bf16)
            cross2(e).start()

    for k in range(1, ns):
        share(k, lax.rem(s + ns - k, ns)).wait_recv()

    def own(i, carry):
        for j in range(C):
            values = coarse_all[aggregate[i, j]]
            spread = jnp.concatenate(
                [jnp.broadcast_to(values[f:f + 1], (width // 4, sides)) for f in range(4)], axis=0)
            out[i, j] = fix_of(i + W, j + W) + spread
        return carry

    lax.fori_loop(0, R, own, 0, unroll=True)

    for d in range(2):
        when(s_has[1 - d], lambda: stream2(d).wait_recv())
    for e in range(2):
        when(c_has[1 - e], lambda: cross2(e).wait_recv())

    def finish(i, carry):
        for j in range(C):
            value = out[i, j] + rs[i, j + W].astype(f32)
            if j < W:
                value = value + rc[i, j].astype(f32)
            if j >= C - W:
                value = value + rc[i, j - C + 2 * W].astype(f32)
            keep = jnp.full(value.shape, i * C + j, jnp.int32) < live
            out[i, j] = jnp.where(keep, value, 0.0)
        return carry

    lax.fori_loop(0, R, finish, 0, unroll=True)

    for e in range(2):
        @pl.when(c_has[e])
        def _():
            cross1(e).wait_send()
            cross2(e).wait_send()
    for d in range(2):
        @pl.when(s_has[d])
        def _():
            stream1(d).wait_send()
            stream2(d).wait_send()
            for e in range(2):
                @pl.when(c_has[e])
                def _():
                    corner1(d, e).wait_send()
                    corner2(d, e).wait_send()
    for k in range(1, ns):
        give(k).wait_send()
        share(k, s).wait_send()


def body(ns, nc, residual, approx_inverse, pattern, live_blocks, block_aggregate, coarse_inverse):
    R, C, width, sides = residual.shape
    _, extent, _, depth = approx_inverse.shape
    owned = coarse_inverse.shape[0] // 4
    bf16, f32 = jnp.bfloat16, jnp.float32
    dma = pltpu.SemaphoreType.DMA
    hbm = pl.BlockSpec(memory_space=pl.ANY)
    smem = pl.BlockSpec(memory_space=pltpu.SMEM)
    vmem = pl.BlockSpec(memory_space=pltpu.VMEM)
    RE, CE = R + 2 * W, C + 2 * W
    return pl.pallas_call(
        functools.partial(kernel, ns, nc, R, C),
        out_shape=jax.ShapeDtypeStruct(residual.shape, f32),
        in_specs=[hbm, hbm, smem, smem, smem, vmem],
        out_specs=vmem,
        scratch_shapes=[
            pltpu.VMEM(residual.shape, bf16),
            pltpu.VMEM((extent, width, depth), bf16),
            pltpu.VMEM((RE, CE, width, sides), bf16),
            pltpu.VMEM((RE, CE, width, sides), bf16),
            pltpu.VMEM((2 * W, CE, width, sides), bf16),
            pltpu.VMEM((R, 2 * W, width, sides), bf16),
            pltpu.VMEM((R, 2 * W, width, sides), bf16),
            pltpu.VMEM((R * C * 4, sides), f32),
            pltpu.VMEM((ns, 4 * owned, sides), f32),
            pltpu.VMEM((ns - 1, 4 * owned, sides), f32),
            pltpu.VMEM((ns * owned, 4, sides), f32),
            dma((2,)),
            dma((4,)), dma((4,)), dma((4,)), dma((4,)),
            dma((ns - 1,)), dma((ns - 1,)), dma((ns - 1,)), dma((ns - 1,)),
            dma((4,)), dma((4,)), dma((4,)), dma((4,)),
        ],
        compiler_params=pltpu.CompilerParams(
            collective_id=0, has_side_effects=True, vmem_limit_bytes=40 * 1024 * 1024),
        cost_estimate=pl.CostEstimate(
            flops=2 * extent * width * depth * sides,
            bytes_accessed=extent * width * depth * 2 + residual.size * 6,
            transcendentals=0),
    )(residual, approx_inverse, pattern, live_blocks, block_aggregate, coarse_inverse)


def solution(mesh):
    placed = (
        P("stream", "cross", None, None),
        P("stream", "cross", None, None),
        P("stream", "cross", None),
        P("stream", "cross"),
        P("stream", "cross"),
        P("stream", "cross"),
    )
    return jax.shard_map(
        functools.partial(body, mesh.shape["stream"], mesh.shape["cross"]),
        mesh=mesh,
        in_specs=placed,
        out_specs=P("stream", "cross", None, None),
        check_vma=False,
    )
```

```python
import functools

import jax
import jax.numpy as jnp
from jax import lax
from jax.experimental import pallas as pl
from jax.experimental.pallas import tpu as pltpu
from jax.sharding import PartitionSpec as P

W = 2


def kernel(
    ns, nc, R, C,
    residual, inverse, pattern_in, live_in, aggregate_in, coarse_in,
    out,
    res, a_mat, pattern, live_ref, aggregate, coarse_inv,
    ext4, fix4, rs, rc, msum, pb, partial, part_in, coarse_all,
    in_sem, h_send, h_recv, t_send, t_recv, q_send, q_recv, p_send, p_recv, g_send, g_recv,
    b_send, b_recv, d_send, d_recv, m_send, m_recv,
):
    s = lax.axis_index("stream")
    c = lax.axis_index("cross")
    width, sides = res.shape[2], res.shape[3]
    CE = C + 2 * W
    RE = R + 2 * W
    owned = coarse_inv.shape[0] // 4
    bf16, f32 = jnp.bfloat16, jnp.float32

    far = lax.rem(s, 2)
    near = 1 - far

    def s_has(d):
        to = s + 2 * d - 1
        return (to >= 0) & (to < ns)

    def c_has(e):
        return c > 0 if e == 0 else c < nc - 1

    def s_to(d):
        return {"stream": jnp.clip(s + 2 * d - 1, 0, ns - 1)}

    def c_to(e):
        return {"cross": jnp.clip(c + 2 * e - 1, 0, nc - 1)}

    loads = [
        pltpu.make_async_copy(residual, res, in_sem.at[0]),
        pltpu.make_async_copy(live_in, live_ref, in_sem.at[1]),
        pltpu.make_async_copy(aggregate_in, aggregate, in_sem.at[2]),
        pltpu.make_async_copy(coarse_in, coarse_inv, in_sem.at[3]),
        pltpu.make_async_copy(pattern_in, pattern, in_sem.at[4]),
        pltpu.make_async_copy(inverse.at[0], a_mat, in_sem.at[5]),
    ]
    for load in loads:
        load.start()

    barrier = pltpu.get_barrier_semaphore()
    for e in range(2):
        @pl.when(c_has(e))
        def _():
            pl.semaphore_signal(barrier, inc=1, device_id=c_to(e),
                                device_id_type=pl.DeviceIdType.MESH)
    for k in range(1, ns):
        pl.semaphore_signal(barrier, inc=1, device_id={"stream": lax.rem(s + k, ns)},
                            device_id_type=pl.DeviceIdType.MESH)

    def zero(ref, rows, cols):
        ref[rows[0]:rows[1], cols[0]:cols[1]] = jnp.zeros(
            (rows[1] - rows[0], cols[1] - cols[0], width, sides), bf16)

    @pl.when(s == 0)
    def _():
        zero(ext4, (0, W), (0, CE))
        zero(rs, (0, W), (0, CE))

    @pl.when(s == ns - 1)
    def _():
        zero(ext4, (R + W, RE), (0, CE))
        zero(rs, (W, 2 * W), (0, CE))

    @pl.when(c == 0)
    def _():
        zero(ext4, (0, RE), (0, W))
        zero(rc, (0, R), (0, W))

    @pl.when(c == nc - 1)
    def _():
        zero(ext4, (0, RE), (C + W, CE))
        zero(rc, (0, R), (W, 2 * W))

    loads[1].wait()
    live = live_ref[0, 0]
    loads[0].wait()

    def mask_row(i, carry):
        for j in range(C):
            block = res[i, j]
            keep = jnp.full(block.shape, i * C + j, jnp.int32) < live
            ext4[i + W, j + W] = jnp.where(keep, block.astype(f32), 0.0).astype(bf16)
        return carry

    lax.fori_loop(0, R, mask_row, 0, unroll=True)

    own_cols = (pl.ds(W, W), pl.ds(C, W))
    halo_cols = (pl.ds(C + W, W), pl.ds(0, W))
    side_cols = (pl.ds(0, W), pl.ds(C + W, W))
    mid_cols = pl.ds(W, C)

    def remote(src, dst, send, recv, to):
        return pltpu.make_async_remote_copy(
            src_ref=src, dst_ref=dst, send_sem=send, recv_sem=recv,
            device_id=to, device_id_type=pl.DeviceIdType.MESH)

    def own_rows(d):
        return pl.ds(W + W * d, W)

    def halo_rows(d):
        return pl.ds((1 - d) * (R + W), W)

    def cross1(e, d):
        i = 2 * e + d
        return remote(ext4.at[own_rows(d), own_cols[e]], ext4.at[own_rows(d), halo_cols[e]],
                      h_send.at[i], h_recv.at[i], c_to(e))

    def stream1(d):
        return remote(ext4.at[own_rows(d), mid_cols], ext4.at[halo_rows(d), mid_cols],
                      t_send.at[d], t_recv.at[d], s_to(d))

    def corner1(d, e):
        i = 2 * e + d
        return remote(ext4.at[own_rows(d), side_cols[e]], ext4.at[halo_rows(d), side_cols[e]],
                      q_send.at[i], q_recv.at[i], s_to(d))

    def far_rows(d):
        return pl.ds(d * (R + W), W)

    def corner2(d, e):
        i = 2 * e + d
        return remote(fix4.at[far_rows(d), side_cols[e]], rs.at[pl.ds(W * (1 - d), W), side_cols[e]],
                      b_send.at[i], b_recv.at[i], s_to(d))

    def stream2(d):
        return remote(fix4.at[far_rows(d), mid_cols], rs.at[pl.ds(W * (1 - d), W), mid_cols],
                      d_send.at[d], d_recv.at[d], s_to(d))

    def cross2(e, d):
        i = 2 * e + d
        return remote(msum.at[pl.ds(W * d, W), pl.ds(W * e, W)],
                      rc.at[pl.ds(W * d, W), pl.ds(W * (1 - e), W)],
                      m_send.at[i], m_recv.at[i], c_to(e))

    def when(cond, run):
        pl.when(cond)(run)

    pl.semaphore_wait(barrier, ns - 1 + c_has(0).astype(jnp.int32) + c_has(1).astype(jnp.int32))

    for d in (far, near):
        for e in range(2):
            when(c_has(e), lambda: cross1(e, d).start())
        when(s_has(d), lambda: stream1(d).start())

    def sums(m, carry):
        i = m // (C // 2)
        j = (m % (C // 2)) * 2
        rows = []
        for t in range(2):
            block = ext4[i + W, j + W + t].astype(f32)
            rows.append(block.reshape(4, width // 4, sides).sum(axis=1))
        pb[pl.ds(pl.multiple_of(m * 8, 8), 8), :] = jnp.concatenate(rows, axis=0)
        return carry

    lax.fori_loop(0, R * C // 2, sums, 0, unroll=True)
    loads[2].wait()
    n_own = R * C
    lane = lax.broadcasted_iota(jnp.int32, (8, 4 * n_own), 1)
    key = jnp.zeros((8, 4 * n_own), jnp.int32)
    for i in range(R):
        for j in range(C):
            key = jnp.where(lane // 4 == i * C + j, aggregate[i, j], key)
    key = (key * 4 + lane % 4)[0:1]
    for o in range(ns):
        row = lax.broadcasted_iota(jnp.int32, (4 * owned, 4 * n_own), 0) + o * 4 * owned
        chosen = (row == jnp.broadcast_to(key, row.shape)).astype(f32)
        partial[o] = jnp.dot(chosen, pb[...], precision=lax.Precision.HIGHEST,
                             preferred_element_type=f32)

    def give(k):
        to = lax.rem(s + k, ns)
        return remote(partial.at[to], part_in.at[k - 1], p_send.at[k - 1], p_recv.at[k - 1],
                      {"stream": to})

    def share(k, mine):
        part = coarse_all.at[pl.ds(mine * owned, owned)]
        return remote(part, part, g_send.at[k - 1], g_recv.at[k - 1],
                      {"stream": lax.rem(s + k, ns)})

    for k in range(1, ns):
        give(k).start()

    for e in range(2):
        when(c_has(1 - e), lambda: cross1(e, far).wait_recv())
    for e in range(2):
        when(s_has(far) & c_has(e), lambda: corner1(far, e).start())

    loads[3].wait()
    total = partial[s]
    for k in range(1, ns):
        give(k).wait_recv()
        total = total + part_in[k - 1]
    coarse = jnp.dot(coarse_inv[...], total, precision=lax.Precision.HIGHEST,
                     preferred_element_type=f32)
    for a in range(owned):
        coarse_all[s * owned + a] = coarse[4 * a:4 * a + 4]
    for k in range(1, ns):
        share(k, s).start()

    for e in range(2):
        when(c_has(1 - e), lambda: cross1(e, near).wait_recv())
    for e in range(2):
        when(s_has(near) & c_has(e), lambda: corner1(near, e).start())

    loads[4].wait()
    loads[5].wait()
    for d in range(2):
        when(s_has(1 - d), lambda: stream1(d).wait_recv())
    for d in (near, far):
        for e in range(2):
            when(s_has(1 - d) & c_has(e), lambda: corner1(d, e).wait_recv())

    ext = ext4.reshape(RE * CE, width, sides)

    def fix_of(i, j):
        n = i * CE + j
        picked = jnp.concatenate(
            [ext[pattern[0, k, n]] for k in range(a_mat.shape[2] // width)], axis=0)
        return jnp.dot(a_mat[n], picked, preferred_element_type=f32)

    edge = tuple(range(W)) + tuple(range(C + W, CE))
    middle = tuple(range(W, C + W))

    def sweep(first, cols):
        def one(t, carry):
            for j in cols:
                fix4[first + t, j] = fix_of(first + t, j).astype(bf16)
            return carry

        lax.fori_loop(0, W, one, 0, unroll=True)

    def fold(d):
        for e in range(2):
            @pl.when(c_has(e))
            def _():
                when(s_has(d), lambda: corner2(1 - d, e).wait_recv())
                for t in range(W):
                    i = W * d + t
                    for j in range(W):
                        col = e * (C + W) + j
                        msum[i, e * W + j] = (
                            fix4[i + W, col].astype(f32) + rs[i, col].astype(f32)).astype(bf16)
                cross2(e, d).start()

    for d in (far, near):
        sweep(d * (R + W), edge)
        for e in range(2):
            when(s_has(d) & c_has(e), lambda: corner2(d, e).start())
    sweep(W + W * near, edge)
    fold(near)
    sweep(W + W * far, edge)
    for d in (far, near):
        sweep(d * (R + W), middle)
        when(s_has(d), lambda: stream2(d).start())
    fold(far)

    for k in range(1, ns):
        share(k, lax.rem(s + ns - k, ns)).wait_recv()

    def own(i, carry):
        for j in range(C):
            values = coarse_all[aggregate[i, j]]
            spread = jnp.concatenate(
                [jnp.broadcast_to(values[f:f + 1], (width // 4, sides)) for f in range(4)], axis=0)
            out[i, j] = fix_of(i + W, j + W) + spread
        return carry

    lax.fori_loop(0, R, own, 0, unroll=True)

    for d in range(2):
        when(s_has(1 - d), lambda: stream2(d).wait_recv())

    def kept(i, j, value):
        keep = jnp.full(value.shape, i * C + j, jnp.int32) < live
        return jnp.where(keep, value, 0.0)

    def add_stream(i, carry):
        for j in range(C):
            out[i, j] = kept(i, j, out[i, j] + rs[i, j + W].astype(f32))
        return carry

    lax.fori_loop(0, R, add_stream, 0, unroll=True)

    def add_cross(d):
        for e in range(2):
            when(c_has(1 - e), lambda: cross2(e, d).wait_recv())
        for t in range(W):
            i = W * d + t
            for j in range(W):
                for col, at in ((j, j), (C - W + j, W + j)):
                    out[i, col] = kept(i, col, out[i, col] + rc[i, at].astype(f32))

    add_cross(near)
    add_cross(far)

    for e in range(2):
        @pl.when(c_has(e))
        def _():
            for d in range(2):
                cross1(e, d).wait_send()
                cross2(e, d).wait_send()
    for d in range(2):
        @pl.when(s_has(d))
        def _():
            stream1(d).wait_send()
            stream2(d).wait_send()
            for e in range(2):
                @pl.when(c_has(e))
                def _():
                    corner1(d, e).wait_send()
                    corner2(d, e).wait_send()
    for k in range(1, ns):
        give(k).wait_send()
        share(k, s).wait_send()


def body(ns, nc, residual, approx_inverse, pattern, live_blocks, block_aggregate, coarse_inverse):
    R, C, width, sides = residual.shape
    _, extent, _, depth = approx_inverse.shape
    owned = coarse_inverse.shape[0] // 4
    bf16, f32, i32 = jnp.bfloat16, jnp.float32, jnp.int32
    dma = pltpu.SemaphoreType.DMA
    hbm = pl.BlockSpec(memory_space=pltpu.HBM)
    vmem = pl.BlockSpec(memory_space=pltpu.VMEM)
    RE, CE = R + 2 * W, C + 2 * W
    links = jnp.transpose(pattern, (0, 2, 1))
    return pl.pallas_call(
        functools.partial(kernel, ns, nc, R, C),
        out_shape=jax.ShapeDtypeStruct(residual.shape, f32),
        in_specs=[hbm] * 6,
        out_specs=vmem,
        scratch_shapes=[
            pltpu.VMEM(residual.shape, bf16),
            pltpu.VMEM((extent, width, depth), bf16),
            pltpu.SMEM(links.shape, i32),
            pltpu.SMEM(live_blocks.shape, i32),
            pltpu.SMEM(block_aggregate.shape, i32),
            pltpu.VMEM(coarse_inverse.shape, f32),
            pltpu.VMEM((RE, CE, width, sides), bf16),
            pltpu.VMEM((RE, CE, width, sides), bf16),
            pltpu.VMEM((2 * W, CE, width, sides), bf16),
            pltpu.VMEM((R, 2 * W, width, sides), bf16),
            pltpu.VMEM((R, 2 * W, width, sides), bf16),
            pltpu.VMEM((R * C * 4, sides), f32),
            pltpu.VMEM((ns, 4 * owned, sides), f32),
            pltpu.VMEM((ns - 1, 4 * owned, sides), f32),
            pltpu.VMEM((ns * owned, 4, sides), f32),
            dma((6,)),
            dma((4,)), dma((4,)), dma((2,)), dma((2,)), dma((4,)), dma((4,)),
            dma((ns - 1,)), dma((ns - 1,)), dma((ns - 1,)), dma((ns - 1,)),
            dma((4,)), dma((4,)), dma((2,)), dma((2,)), dma((4,)), dma((4,)),
        ],
        compiler_params=pltpu.CompilerParams(
            collective_id=0, has_side_effects=True, vmem_limit_bytes=60 * 1024 * 1024),
        cost_estimate=pl.CostEstimate(
            flops=2 * extent * width * depth * sides,
            bytes_accessed=extent * width * depth * 2 + residual.size * 6,
            transcendentals=0),
    )(residual, approx_inverse, links, live_blocks, block_aggregate, coarse_inverse)


def solution(mesh):
    placed = (
        P("stream", "cross", None, None),
        P("stream", "cross", None, None),
        P("stream", "cross", None),
        P("stream", "cross"),
        P("stream", "cross"),
        P("stream", "cross"),
    )
    return jax.shard_map(
        functools.partial(body, mesh.shape["stream"], mesh.shape["cross"]),
        mesh=mesh,
        in_specs=placed,
        out_specs=P("stream", "cross", None, None),
        check_vma=False,
    )
```

```python
import functools

import jax
import jax.numpy as jnp
from jax import lax
from jax.experimental import pallas as pl
from jax.experimental.pallas import tpu as pltpu
from jax.sharding import PartitionSpec as P

W = 2


def kernel(
    ns, nc, R, C,
    live_ref, residual, inverse, pattern_in, aggregate_in, coarse_in,
    out,
    res, a_mat, pattern, aggregate, coarse_inv,
    ext4, fix4, rs, rc, msum, pb, partial, part_in, coarse_all,
    in_sem, h_send, h_recv, t_send, t_recv, q_send, q_recv, p_send, p_recv, g_send, g_recv,
    b_send, b_recv, d_send, d_recv, m_send, m_recv,
):
    s = lax.axis_index("stream")
    c = lax.axis_index("cross")
    width, sides = res.shape[2], res.shape[3]
    CE = C + 2 * W
    RE = R + 2 * W
    owned = coarse_inv.shape[0] // 4
    bf16, f32 = jnp.bfloat16, jnp.float32

    far = lax.rem(s, 2)
    near = 1 - far

    def s_has(d):
        to = s + 2 * d - 1
        return (to >= 0) & (to < ns)

    def c_has(e):
        return c > 0 if e == 0 else c < nc - 1

    def s_to(d):
        return {"stream": jnp.clip(s + 2 * d - 1, 0, ns - 1)}

    def c_to(e):
        return {"cross": jnp.clip(c + 2 * e - 1, 0, nc - 1)}

    loads = [
        pltpu.make_async_copy(residual, res, in_sem.at[0]),
        pltpu.make_async_copy(aggregate_in, aggregate, in_sem.at[1]),
        pltpu.make_async_copy(coarse_in, coarse_inv, in_sem.at[2]),
        pltpu.make_async_copy(pattern_in, pattern, in_sem.at[3]),
        pltpu.make_async_copy(inverse.at[0], a_mat, in_sem.at[4]),
    ]
    for load in loads:
        load.start()

    barrier = pltpu.get_barrier_semaphore()
    for e in range(2):
        @pl.when(c_has(e))
        def _():
            pl.semaphore_signal(barrier, inc=1, device_id=c_to(e),
                                device_id_type=pl.DeviceIdType.MESH)
    for k in range(1, ns):
        pl.semaphore_signal(barrier, inc=1, device_id={"stream": lax.rem(s + k, ns)},
                            device_id_type=pl.DeviceIdType.MESH)

    def zero(ref, rows, cols):
        ref[rows[0]:rows[1], cols[0]:cols[1]] = jnp.zeros(
            (rows[1] - rows[0], cols[1] - cols[0], width, sides), bf16)

    @pl.when(s == 0)
    def _():
        zero(ext4, (0, W), (0, CE))
        zero(rs, (0, W), (0, CE))

    @pl.when(s == ns - 1)
    def _():
        zero(ext4, (R + W, RE), (0, CE))
        zero(rs, (W, 2 * W), (0, CE))

    @pl.when(c == 0)
    def _():
        zero(ext4, (0, RE), (0, W))
        zero(rc, (0, R), (0, W))

    @pl.when(c == nc - 1)
    def _():
        zero(ext4, (0, RE), (C + W, CE))
        zero(rc, (0, R), (W, 2 * W))

    live = live_ref[0, 0]
    loads[0].wait()

    def mask(cols):
        def row(i, carry):
            for j in cols:
                block = res[i, j]
                keep = jnp.full(block.shape, i * C + j, jnp.int32) < live
                ext4[i + W, j + W] = jnp.where(keep, block.astype(f32), 0.0).astype(bf16)
            return carry

        lax.fori_loop(0, R, row, 0, unroll=True)

    mask(tuple(range(W)) + tuple(range(C - W, C)))

    own_cols = (pl.ds(W, W), pl.ds(C, W))
    halo_cols = (pl.ds(C + W, W), pl.ds(0, W))
    side_cols = (pl.ds(0, W), pl.ds(C + W, W))
    mid_cols = pl.ds(W, C)

    def remote(src, dst, send, recv, to):
        return pltpu.make_async_remote_copy(
            src_ref=src, dst_ref=dst, send_sem=send, recv_sem=recv,
            device_id=to, device_id_type=pl.DeviceIdType.MESH)

    def own_rows(d):
        return pl.ds(W + W * d, W)

    def halo_rows(d):
        return pl.ds((1 - d) * (R + W), W)

    def cross1(e, d):
        i = 2 * e + d
        return remote(ext4.at[own_rows(d), own_cols[e]], ext4.at[own_rows(d), halo_cols[e]],
                      h_send.at[i], h_recv.at[i], c_to(e))

    def stream1(d):
        return remote(ext4.at[own_rows(d), mid_cols], ext4.at[halo_rows(d), mid_cols],
                      t_send.at[d], t_recv.at[d], s_to(d))

    def corner1(d, e):
        i = 2 * e + d
        return remote(ext4.at[own_rows(d), side_cols[e]], ext4.at[halo_rows(d), side_cols[e]],
                      q_send.at[i], q_recv.at[i], s_to(d))

    def far_rows(d):
        return pl.ds(d * (R + W), W)

    def corner2(d, e):
        i = 2 * e + d
        return remote(fix4.at[far_rows(d), side_cols[e]], rs.at[pl.ds(W * (1 - d), W), side_cols[e]],
                      b_send.at[i], b_recv.at[i], s_to(d))

    def stream2(d):
        return remote(fix4.at[far_rows(d), mid_cols], rs.at[pl.ds(W * (1 - d), W), mid_cols],
                      d_send.at[d], d_recv.at[d], s_to(d))

    def cross2(e, d):
        i = 2 * e + d
        return remote(msum.at[pl.ds(W * d, W), pl.ds(W * e, W)],
                      rc.at[pl.ds(W * d, W), pl.ds(W * (1 - e), W)],
                      m_send.at[i], m_recv.at[i], c_to(e))

    def when(cond, run):
        pl.when(cond)(run)

    pl.semaphore_wait(barrier, ns - 1 + c_has(0).astype(jnp.int32) + c_has(1).astype(jnp.int32))

    for d in (far, near):
        for e in range(2):
            when(c_has(e), lambda: cross1(e, d).start())
    mask(range(W, C - W))
    for d in (far, near):
        when(s_has(d), lambda: stream1(d).start())

    def sums(m, carry):
        i = m // (C // 2)
        j = (m % (C // 2)) * 2
        rows = []
        for t in range(2):
            block = ext4[i + W, j + W + t].astype(f32)
            rows.append(block.reshape(4, width // 4, sides).sum(axis=1))
        pb[pl.ds(pl.multiple_of(m * 8, 8), 8), :] = jnp.concatenate(rows, axis=0)
        return carry

    lax.fori_loop(0, R * C // 2, sums, 0, unroll=True)
    loads[1].wait()
    n_own = R * C
    lane = lax.broadcasted_iota(jnp.int32, (8, 4 * n_own), 1)
    key = jnp.zeros((8, 4 * n_own), jnp.int32)
    for i in range(R):
        for j in range(C):
            key = jnp.where(lane // 4 == i * C + j, aggregate[i, j], key)
    key = (key * 4 + lane % 4)[0:1]
    for o in range(ns):
        row = lax.broadcasted_iota(jnp.int32, (4 * owned, 4 * n_own), 0) + o * 4 * owned
        chosen = (row == jnp.broadcast_to(key, row.shape)).astype(f32)
        partial[o] = jnp.dot(chosen, pb[...], precision=lax.Precision.HIGHEST,
                             preferred_element_type=f32)

    def give(k):
        to = lax.rem(s + k, ns)
        return remote(partial.at[to], part_in.at[k - 1], p_send.at[k - 1], p_recv.at[k - 1],
                      {"stream": to})

    def share(k, mine):
        part = coarse_all.at[pl.ds(mine * owned, owned)]
        return remote(part, part, g_send.at[k - 1], g_recv.at[k - 1],
                      {"stream": lax.rem(s + k, ns)})

    for k in range(1, ns):
        give(k).start()

    for e in range(2):
        when(c_has(1 - e), lambda: cross1(e, far).wait_recv())
    for e in range(2):
        when(s_has(far) & c_has(e), lambda: corner1(far, e).start())

    loads[2].wait()
    total = partial[s]
    for k in range(1, ns):
        give(k).wait_recv()
        total = total + part_in[k - 1]
    coarse = jnp.dot(coarse_inv[...], total, precision=lax.Precision.HIGHEST,
                     preferred_element_type=f32)
    for a in range(owned):
        coarse_all[s * owned + a] = coarse[4 * a:4 * a + 4]
    for k in range(1, ns):
        share(k, s).start()

    for e in range(2):
        when(c_has(1 - e), lambda: cross1(e, near).wait_recv())
    for e in range(2):
        when(s_has(near) & c_has(e), lambda: corner1(near, e).start())

    loads[3].wait()
    loads[4].wait()
    for d in range(2):
        when(s_has(1 - d), lambda: stream1(d).wait_recv())
    for d in (near, far):
        for e in range(2):
            when(s_has(1 - d) & c_has(e), lambda: corner1(d, e).wait_recv())

    ext = ext4.reshape(RE * CE, width, sides)

    def fix_of(i, j):
        n = i * CE + j
        picked = jnp.concatenate(
            [ext[pattern[0, k, n]] for k in range(a_mat.shape[2] // width)], axis=0)
        return jnp.dot(a_mat[n], picked, preferred_element_type=f32)

    edge = tuple(range(W)) + tuple(range(C + W, CE))
    middle = tuple(range(W, C + W))

    def sweep(first, cols):
        def one(t, carry):
            for j in cols:
                fix4[first + t, j] = fix_of(first + t, j).astype(bf16)
            return carry

        lax.fori_loop(0, W, one, 0, unroll=True)

    def fold(d):
        for e in range(2):
            @pl.when(c_has(e))
            def _():
                when(s_has(d), lambda: corner2(1 - d, e).wait_recv())
                for t in range(W):
                    i = W * d + t
                    for j in range(W):
                        col = e * (C + W) + j
                        msum[i, e * W + j] = (
                            fix4[i + W, col].astype(f32) + rs[i, col].astype(f32)).astype(bf16)
                cross2(e, d).start()

    for d in (near, far):
        sweep(d * (R + W), edge)
        for e in range(2):
            when(s_has(d) & c_has(e), lambda: corner2(d, e).start())
    sweep(W + W * near, edge)
    fold(near)
    sweep(W + W * far, edge)
    sweep(far * (R + W), middle)
    when(s_has(far), lambda: stream2(far).start())
    fold(far)
    sweep(near * (R + W), middle)
    when(s_has(near), lambda: stream2(near).start())

    for k in range(1, ns):
        share(k, lax.rem(s + ns - k, ns)).wait_recv()

    def own(i, carry):
        for j in range(C):
            values = coarse_all[aggregate[i, j]]
            spread = jnp.concatenate(
                [jnp.broadcast_to(values[f:f + 1], (width // 4, sides)) for f in range(4)], axis=0)
            out[i, j] = fix_of(i + W, j + W) + spread
        return carry

    lax.fori_loop(0, R, own, 0, unroll=True)

    for d in range(2):
        when(s_has(1 - d), lambda: stream2(d).wait_recv())

    def kept(i, j, value):
        keep = jnp.full(value.shape, i * C + j, jnp.int32) < live
        return jnp.where(keep, value, 0.0)

    def add_stream(i, carry):
        for j in range(C):
            out[i, j] = kept(i, j, out[i, j] + rs[i, j + W].astype(f32))
        return carry

    lax.fori_loop(0, R, add_stream, 0, unroll=True)

    def add_cross(d):
        for e in range(2):
            when(c_has(1 - e), lambda: cross2(e, d).wait_recv())
        for t in range(W):
            i = W * d + t
            for j in range(W):
                for col, at in ((j, j), (C - W + j, W + j)):
                    out[i, col] = kept(i, col, out[i, col] + rc[i, at].astype(f32))

    add_cross(near)
    add_cross(far)

    for e in range(2):
        @pl.when(c_has(e))
        def _():
            for d in range(2):
                cross1(e, d).wait_send()
                cross2(e, d).wait_send()
    for d in range(2):
        @pl.when(s_has(d))
        def _():
            stream1(d).wait_send()
            stream2(d).wait_send()
            for e in range(2):
                @pl.when(c_has(e))
                def _():
                    corner1(d, e).wait_send()
                    corner2(d, e).wait_send()
    for k in range(1, ns):
        give(k).wait_send()
        share(k, s).wait_send()


def body(ns, nc, residual, approx_inverse, pattern, live_blocks, block_aggregate, coarse_inverse):
    R, C, width, sides = residual.shape
    _, extent, _, depth = approx_inverse.shape
    owned = coarse_inverse.shape[0] // 4
    bf16, f32, i32 = jnp.bfloat16, jnp.float32, jnp.int32
    dma = pltpu.SemaphoreType.DMA
    hbm = pl.BlockSpec(memory_space=pltpu.HBM)
    vmem = pl.BlockSpec(memory_space=pltpu.VMEM)
    RE, CE = R + 2 * W, C + 2 * W
    links = jnp.transpose(pattern, (0, 2, 1))
    operands = (residual, approx_inverse, links, block_aggregate, coarse_inverse)
    return pl.pallas_call(
        functools.partial(kernel, ns, nc, R, C),
        out_shape=pltpu.VMEM(residual.shape, f32),
        in_specs=[pl.BlockSpec(memory_space=pltpu.SMEM)] + [hbm] * 5,
        out_specs=vmem,
        scratch_shapes=[
            pltpu.VMEM(residual.shape, bf16),
            pltpu.VMEM((extent, width, depth), bf16),
            pltpu.SMEM(links.shape, i32),
            pltpu.SMEM(block_aggregate.shape, i32),
            pltpu.VMEM(coarse_inverse.shape, f32),
            pltpu.VMEM((RE, CE, width, sides), bf16),
            pltpu.VMEM((RE, CE, width, sides), bf16),
            pltpu.VMEM((2 * W, CE, width, sides), bf16),
            pltpu.VMEM((R, 2 * W, width, sides), bf16),
            pltpu.VMEM((R, 2 * W, width, sides), bf16),
            pltpu.VMEM((R * C * 4, sides), f32),
            pltpu.VMEM((ns, 4 * owned, sides), f32),
            pltpu.VMEM((ns - 1, 4 * owned, sides), f32),
            pltpu.VMEM((ns * owned, 4, sides), f32),
            dma((5,)),
            dma((4,)), dma((4,)), dma((2,)), dma((2,)), dma((4,)), dma((4,)),
            dma((ns - 1,)), dma((ns - 1,)), dma((ns - 1,)), dma((ns - 1,)),
            dma((4,)), dma((4,)), dma((2,)), dma((2,)), dma((4,)), dma((4,)),
        ],
        compiler_params=pltpu.CompilerParams(
            collective_id=0, has_side_effects=True, vmem_limit_bytes=40 * 1024 * 1024),
        cost_estimate=pl.CostEstimate(
            flops=2 * extent * width * depth * sides,
            bytes_accessed=extent * width * depth * 2 + residual.size * 6,
            transcendentals=0),
    )(live_blocks, *(pltpu.with_memory_space_constraint(array, pltpu.HBM) for array in operands))


def solution(mesh):
    placed = (
        P("stream", "cross", None, None),
        P("stream", "cross", None, None),
        P("stream", "cross", None),
        P("stream", "cross"),
        P("stream", "cross"),
        P("stream", "cross"),
    )
    return jax.shard_map(
        functools.partial(body, mesh.shape["stream"], mesh.shape["cross"]),
        mesh=mesh,
        in_specs=placed,
        out_specs=P("stream", "cross", None, None),
        check_vma=False,
    )
```

```python
import functools

import jax
import jax.numpy as jnp
from jax import lax
from jax.experimental import pallas as pl
from jax.experimental.pallas import tpu as pltpu
from jax.sharding import PartitionSpec as P

W = 2


def kernel(
    ns, nc, R, C,
    live_ref, residual, inverse, pattern_in, aggregate_in, coarse_in,
    out,
    res, a_mat, pattern, aggregate, coarse_inv,
    ext4, fix4, rs, rc, msum, pb, partial, part_in, coarse_all,
    in_sem, h_send, h_recv, t_send, t_recv, q_send, q_recv, p_send, p_recv, g_send, g_recv,
    b_send, b_recv, d_send, d_recv, m_send, m_recv,
):
    s = lax.axis_index("stream")
    c = lax.axis_index("cross")
    width, sides = res.shape[2], res.shape[3]
    CE = C + 2 * W
    RE = R + 2 * W
    owned = coarse_inv.shape[0] // 4
    bf16, f32 = jnp.bfloat16, jnp.float32

    far = lax.rem(s, 2)
    near = 1 - far

    def s_has(d):
        to = s + 2 * d - 1
        return (to >= 0) & (to < ns)

    def c_has(e):
        return c > 0 if e == 0 else c < nc - 1

    def s_to(d):
        return {"stream": jnp.clip(s + 2 * d - 1, 0, ns - 1)}

    def c_to(e):
        return {"cross": jnp.clip(c + 2 * e - 1, 0, nc - 1)}

    loads = [
        pltpu.make_async_copy(residual, res, in_sem.at[0]),
        pltpu.make_async_copy(aggregate_in, aggregate, in_sem.at[1]),
        pltpu.make_async_copy(coarse_in, coarse_inv, in_sem.at[2]),
        pltpu.make_async_copy(pattern_in, pattern, in_sem.at[3]),
        pltpu.make_async_copy(inverse.at[0], a_mat, in_sem.at[4]),
    ]
    for load in loads:
        load.start()

    barrier = pltpu.get_barrier_semaphore()
    for e in range(2):
        @pl.when(c_has(e))
        def _():
            pl.semaphore_signal(barrier, inc=1, device_id=c_to(e),
                                device_id_type=pl.DeviceIdType.MESH)
    for k in range(1, ns):
        pl.semaphore_signal(barrier, inc=1, device_id={"stream": lax.rem(s + k, ns)},
                            device_id_type=pl.DeviceIdType.MESH)

    def zero(ref, rows, cols):
        ref[rows[0]:rows[1], cols[0]:cols[1]] = jnp.zeros(
            (rows[1] - rows[0], cols[1] - cols[0], width, sides), bf16)

    @pl.when(s == 0)
    def _():
        zero(ext4, (0, W), (0, CE))
        zero(rs, (0, W), (0, CE))

    @pl.when(s == ns - 1)
    def _():
        zero(ext4, (R + W, RE), (0, CE))
        zero(rs, (W, 2 * W), (0, CE))

    @pl.when(c == 0)
    def _():
        zero(ext4, (0, RE), (0, W))
        zero(rc, (0, R), (0, W))

    @pl.when(c == nc - 1)
    def _():
        zero(ext4, (0, RE), (C + W, CE))
        zero(rc, (0, R), (W, 2 * W))

    live = live_ref[0, 0]
    loads[0].wait()

    def mask(cols):
        def row(i, carry):
            for j in cols:
                block = res[i, j]
                keep = jnp.full(block.shape, i * C + j, jnp.int32) < live
                ext4[i + W, j + W] = jnp.where(keep, block.astype(f32), 0.0).astype(bf16)
            return carry

        lax.fori_loop(0, R, row, 0, unroll=True)

    mask(tuple(range(W)) + tuple(range(C - W, C)))

    own_cols = (pl.ds(W, W), pl.ds(C, W))
    halo_cols = (pl.ds(C + W, W), pl.ds(0, W))
    side_cols = (pl.ds(0, W), pl.ds(C + W, W))
    mid_cols = pl.ds(W, C)

    def remote(src, dst, send, recv, to):
        return pltpu.make_async_remote_copy(
            src_ref=src, dst_ref=dst, send_sem=send, recv_sem=recv,
            device_id=to, device_id_type=pl.DeviceIdType.MESH)

    def own_rows(d):
        return pl.ds(W + W * d, W)

    def halo_rows(d):
        return pl.ds((1 - d) * (R + W), W)

    def cross1(e, d):
        i = 2 * e + d
        return remote(ext4.at[own_rows(d), own_cols[e]], ext4.at[own_rows(d), halo_cols[e]],
                      h_send.at[i], h_recv.at[i], c_to(e))

    def stream1(d):
        return remote(ext4.at[own_rows(d), mid_cols], ext4.at[halo_rows(d), mid_cols],
                      t_send.at[d], t_recv.at[d], s_to(d))

    def corner1(d, e):
        i = 2 * e + d
        return remote(ext4.at[own_rows(d), side_cols[e]], ext4.at[halo_rows(d), side_cols[e]],
                      q_send.at[i], q_recv.at[i], s_to(d))

    def far_rows(d):
        return pl.ds(d * (R + W), W)

    def corner2(d, e):
        i = 2 * e + d
        return remote(fix4.at[far_rows(d), side_cols[e]], rs.at[pl.ds(W * (1 - d), W), side_cols[e]],
                      b_send.at[i], b_recv.at[i], s_to(d))

    def stream2(d):
        return remote(fix4.at[far_rows(d), mid_cols], rs.at[pl.ds(W * (1 - d), W), mid_cols],
                      d_send.at[d], d_recv.at[d], s_to(d))

    def cross2(e, d):
        i = 2 * e + d
        return remote(msum.at[pl.ds(W * d, W), pl.ds(W * e, W)],
                      rc.at[pl.ds(W * d, W), pl.ds(W * (1 - e), W)],
                      m_send.at[i], m_recv.at[i], c_to(e))

    def when(cond, run):
        pl.when(cond)(run)

    pl.semaphore_wait(barrier, ns - 1 + c_has(0).astype(jnp.int32) + c_has(1).astype(jnp.int32))

    for d in (far, near):
        for e in range(2):
            when(c_has(e), lambda: cross1(e, d).start())
    mask(range(W, C - W))
    for d in (far, near):
        when(s_has(d), lambda: stream1(d).start())

    def sums(m, carry):
        i = m // (C // 2)
        j = (m % (C // 2)) * 2
        rows = []
        for t in range(2):
            block = ext4[i + W, j + W + t].astype(f32)
            rows.append(block.reshape(4, width // 4, sides).sum(axis=1))
        pb[pl.ds(pl.multiple_of(m * 8, 8), 8), :] = jnp.concatenate(rows, axis=0)
        return carry

    lax.fori_loop(0, R * C // 2, sums, 0, unroll=True)
    loads[1].wait()
    n_own = R * C
    lane = lax.broadcasted_iota(jnp.int32, (8, 4 * n_own), 1)
    key = jnp.zeros((8, 4 * n_own), jnp.int32)
    for i in range(R):
        for j in range(C):
            key = jnp.where(lane // 4 == i * C + j, aggregate[i, j], key)
    key = (key * 4 + lane % 4)[0:1]
    row = lax.broadcasted_iota(jnp.int32, (4 * owned * ns, 4 * n_own), 0)
    chosen = (row == jnp.broadcast_to(key, row.shape)).astype(f32)
    restricted = jnp.dot(chosen, pb[...], precision=lax.Precision.HIGHEST,
                         preferred_element_type=f32)
    for o in range(ns):
        partial[o] = restricted[o * 4 * owned:(o + 1) * 4 * owned]

    def give(k):
        to = lax.rem(s + k, ns)
        return remote(partial.at[to], part_in.at[k - 1], p_send.at[k - 1], p_recv.at[k - 1],
                      {"stream": to})

    def share(k, mine):
        part = coarse_all.at[pl.ds(mine * owned, owned)]
        return remote(part, part, g_send.at[k - 1], g_recv.at[k - 1],
                      {"stream": lax.rem(s + k, ns)})

    for k in range(1, ns):
        give(k).start()

    for d in (far, near):
        for e in range(2):
            @pl.when(c_has(1 - e))
            def _():
                cross1(e, d).wait_recv()
                when(s_has(d), lambda: corner1(d, 1 - e).start())

    loads[3].wait()
    loads[4].wait()
    for d in range(2):
        when(s_has(1 - d), lambda: stream1(d).wait_recv())
    for d in (near, far):
        for e in range(2):
            when(s_has(1 - d) & c_has(e), lambda: corner1(d, e).wait_recv())

    ext = ext4.reshape(RE * CE, width, sides)

    def fix_of(i, j):
        n = i * CE + j
        picked = jnp.concatenate(
            [ext[pattern[0, k, n]] for k in range(a_mat.shape[2] // width)], axis=0)
        return jnp.dot(a_mat[n], picked, preferred_element_type=f32)

    edge = tuple(range(W)) + tuple(range(C + W, CE))
    middle = tuple(range(W, C + W))

    def sweep(first, cols):
        def one(t, carry):
            for j in cols:
                fix4[first + t, j] = fix_of(first + t, j).astype(bf16)
            return carry

        lax.fori_loop(0, W, one, 0, unroll=True)

    def fold(d):
        for e in range(2):
            @pl.when(c_has(e))
            def _():
                when(s_has(d), lambda: corner2(1 - d, e).wait_recv())
                for t in range(W):
                    i = W * d + t
                    for j in range(W):
                        col = e * (C + W) + j
                        msum[i, e * W + j] = (
                            fix4[i + W, col].astype(f32) + rs[i, col].astype(f32)).astype(bf16)
                cross2(e, d).start()

    def coarse_step():
        loads[2].wait()
        total = partial[s]
        for k in range(1, ns):
            give(k).wait_recv()
            total = total + part_in[k - 1]
        coarse = jnp.dot(coarse_inv[...], total, precision=lax.Precision.HIGHEST,
                         preferred_element_type=f32)
        for a in range(owned):
            coarse_all[s * owned + a] = coarse[4 * a:4 * a + 4]
        for k in range(1, ns):
            share(k, s).start()

    for d in (near, far):
        sweep(d * (R + W), edge)
        for e in range(2):
            when(s_has(d) & c_has(e), lambda: corner2(d, e).start())
    sweep(W + W * near, edge)
    fold(near)
    coarse_step()
    sweep(W + W * far, edge)
    sweep(far * (R + W), middle)
    when(s_has(far), lambda: stream2(far).start())
    fold(far)
    sweep(near * (R + W), middle)
    when(s_has(near), lambda: stream2(near).start())

    for k in range(1, ns):
        share(k, lax.rem(s + ns - k, ns)).wait_recv()

    def own(i, carry):
        for j in range(C):
            values = coarse_all[aggregate[i, j]]
            spread = jnp.concatenate(
                [jnp.broadcast_to(values[f:f + 1], (width // 4, sides)) for f in range(4)], axis=0)
            out[i, j] = fix_of(i + W, j + W) + spread
        return carry

    lax.fori_loop(0, R, own, 0, unroll=True)

    for d in range(2):
        when(s_has(1 - d), lambda: stream2(d).wait_recv())

    def kept(i, j, value):
        keep = jnp.full(value.shape, i * C + j, jnp.int32) < live
        return jnp.where(keep, value, 0.0)

    def add_stream(i, carry):
        for j in range(C):
            out[i, j] = kept(i, j, out[i, j] + rs[i, j + W].astype(f32))
        return carry

    lax.fori_loop(0, R, add_stream, 0, unroll=True)

    def add_cross(d):
        for e in range(2):
            when(c_has(1 - e), lambda: cross2(e, d).wait_recv())
        for t in range(W):
            i = W * d + t
            for j in range(W):
                for col, at in ((j, j), (C - W + j, W + j)):
                    out[i, col] = kept(i, col, out[i, col] + rc[i, at].astype(f32))

    add_cross(near)
    add_cross(far)

    for e in range(2):
        @pl.when(c_has(e))
        def _():
            for d in range(2):
                cross1(e, d).wait_send()
                cross2(e, d).wait_send()
    for d in range(2):
        @pl.when(s_has(d))
        def _():
            stream1(d).wait_send()
            stream2(d).wait_send()
            for e in range(2):
                @pl.when(c_has(e))
                def _():
                    corner1(d, e).wait_send()
                    corner2(d, e).wait_send()
    for k in range(1, ns):
        give(k).wait_send()
        share(k, s).wait_send()


def body(ns, nc, residual, approx_inverse, pattern, live_blocks, block_aggregate, coarse_inverse):
    R, C, width, sides = residual.shape
    _, extent, _, depth = approx_inverse.shape
    owned = coarse_inverse.shape[0] // 4
    bf16, f32, i32 = jnp.bfloat16, jnp.float32, jnp.int32
    dma = pltpu.SemaphoreType.DMA
    hbm = pl.BlockSpec(memory_space=pltpu.HBM)
    vmem = pl.BlockSpec(memory_space=pltpu.VMEM)
    RE, CE = R + 2 * W, C + 2 * W
    links = jnp.transpose(pattern, (0, 2, 1))
    operands = (residual, approx_inverse, links, block_aggregate, coarse_inverse)
    return pl.pallas_call(
        functools.partial(kernel, ns, nc, R, C),
        out_shape=pltpu.VMEM(residual.shape, f32),
        in_specs=[pl.BlockSpec(memory_space=pltpu.SMEM)] + [hbm] * 5,
        out_specs=vmem,
        scratch_shapes=[
            pltpu.VMEM(residual.shape, bf16),
            pltpu.VMEM((extent, width, depth), bf16),
            pltpu.SMEM(links.shape, i32),
            pltpu.SMEM(block_aggregate.shape, i32),
            pltpu.VMEM(coarse_inverse.shape, f32),
            pltpu.VMEM((RE, CE, width, sides), bf16),
            pltpu.VMEM((RE, CE, width, sides), bf16),
            pltpu.VMEM((2 * W, CE, width, sides), bf16),
            pltpu.VMEM((R, 2 * W, width, sides), bf16),
            pltpu.VMEM((R, 2 * W, width, sides), bf16),
            pltpu.VMEM((R * C * 4, sides), f32),
            pltpu.VMEM((ns, 4 * owned, sides), f32),
            pltpu.VMEM((ns - 1, 4 * owned, sides), f32),
            pltpu.VMEM((ns * owned, 4, sides), f32),
            dma((5,)),
            dma((4,)), dma((4,)), dma((2,)), dma((2,)), dma((4,)), dma((4,)),
            dma((ns - 1,)), dma((ns - 1,)), dma((ns - 1,)), dma((ns - 1,)),
            dma((4,)), dma((4,)), dma((2,)), dma((2,)), dma((4,)), dma((4,)),
        ],
        compiler_params=pltpu.CompilerParams(
            collective_id=0, has_side_effects=True, vmem_limit_bytes=40 * 1024 * 1024),
        cost_estimate=pl.CostEstimate(
            flops=2 * extent * width * depth * sides,
            bytes_accessed=extent * width * depth * 2 + residual.size * 6,
            transcendentals=0),
    )(live_blocks, *(pltpu.with_memory_space_constraint(array, pltpu.HBM) for array in operands))


def solution(mesh):
    placed = (
        P("stream", "cross", None, None),
        P("stream", "cross", None, None),
        P("stream", "cross", None),
        P("stream", "cross"),
        P("stream", "cross"),
        P("stream", "cross"),
    )
    return jax.shard_map(
        functools.partial(body, mesh.shape["stream"], mesh.shape["cross"]),
        mesh=mesh,
        in_specs=placed,
        out_specs=P("stream", "cross", None, None),
        check_vma=False,
    )
```

```python
import functools

import jax
import jax.numpy as jnp
from jax import lax
from jax.experimental import pallas as pl
from jax.experimental.pallas import tpu as pltpu
from jax.sharding import PartitionSpec as P

W = 2


def kernel(
    ns, nc, R, C,
    live_ref, residual, inverse, pattern_in, aggregate_in, coarse_in,
    out,
    res, a_mat, pattern, aggregate, coarse_inv,
    ext4, fix4, rs, rc, msum, pb, partial, part_in, coarse_all,
    in_sem, h_send, h_recv, t_send, t_recv, q_send, q_recv, p_send, p_recv, g_send, g_recv,
    b_send, b_recv, d_send, d_recv, m_send, m_recv,
):
    s = lax.axis_index("stream")
    c = lax.axis_index("cross")
    width, sides = res.shape[2], res.shape[3]
    CE = C + 2 * W
    RE = R + 2 * W
    owned = coarse_inv.shape[0] // 4
    bf16, f32 = jnp.bfloat16, jnp.float32

    far = lax.rem(s, 2)
    near = 1 - far

    def s_has(d):
        to = s + 2 * d - 1
        return (to >= 0) & (to < ns)

    def c_has(e):
        return c > 0 if e == 0 else c < nc - 1

    def s_to(d):
        return {"stream": jnp.clip(s + 2 * d - 1, 0, ns - 1)}

    def c_to(e):
        return {"cross": jnp.clip(c + 2 * e - 1, 0, nc - 1)}

    loads = [
        pltpu.make_async_copy(residual, res, in_sem.at[0]),
        pltpu.make_async_copy(aggregate_in, aggregate, in_sem.at[1]),
        pltpu.make_async_copy(coarse_in, coarse_inv, in_sem.at[2]),
        pltpu.make_async_copy(pattern_in, pattern, in_sem.at[3]),
        pltpu.make_async_copy(inverse.at[0], a_mat, in_sem.at[4]),
    ]
    for load in loads:
        load.start()

    barrier = pltpu.get_barrier_semaphore()
    for e in range(2):
        @pl.when(c_has(e))
        def _():
            pl.semaphore_signal(barrier, inc=1, device_id=c_to(e),
                                device_id_type=pl.DeviceIdType.MESH)
    for k in range(1, ns):
        pl.semaphore_signal(barrier, inc=1, device_id={"stream": lax.rem(s + k, ns)},
                            device_id_type=pl.DeviceIdType.MESH)

    def zero(ref, rows, cols):
        ref[rows[0]:rows[1], cols[0]:cols[1]] = jnp.zeros(
            (rows[1] - rows[0], cols[1] - cols[0], width, sides), bf16)

    @pl.when(s == 0)
    def _():
        zero(ext4, (0, W), (0, CE))
        zero(rs, (0, W), (0, CE))

    @pl.when(s == ns - 1)
    def _():
        zero(ext4, (R + W, RE), (0, CE))
        zero(rs, (W, 2 * W), (0, CE))

    @pl.when(c == 0)
    def _():
        zero(ext4, (0, RE), (0, W))
        zero(rc, (0, R), (0, W))

    @pl.when(c == nc - 1)
    def _():
        zero(ext4, (0, RE), (C + W, CE))
        zero(rc, (0, R), (W, 2 * W))

    live = live_ref[0, 0]
    loads[0].wait()

    def mask(cols):
        def row(i, carry):
            for j in cols:
                block = res[i, j]
                keep = jnp.full(block.shape, i * C + j, jnp.int32) < live
                ext4[i + W, j + W] = jnp.where(keep, block.astype(f32), 0.0).astype(bf16)
            return carry

        lax.fori_loop(0, R, row, 0)

    mask(tuple(range(W)) + tuple(range(C - W, C)))

    own_cols = (pl.ds(W, W), pl.ds(C, W))
    halo_cols = (pl.ds(C + W, W), pl.ds(0, W))
    side_cols = (pl.ds(0, W), pl.ds(C + W, W))
    mid_cols = pl.ds(W, C)

    def remote(src, dst, send, recv, to):
        return pltpu.make_async_remote_copy(
            src_ref=src, dst_ref=dst, send_sem=send, recv_sem=recv,
            device_id=to, device_id_type=pl.DeviceIdType.MESH)

    def own_rows(d):
        return pl.ds(W + W * d, W)

    def halo_rows(d):
        return pl.ds((1 - d) * (R + W), W)

    def cross1(e, d):
        i = 2 * e + d
        return remote(ext4.at[own_rows(d), own_cols[e]], ext4.at[own_rows(d), halo_cols[e]],
                      h_send.at[i], h_recv.at[i], c_to(e))

    def stream1(d):
        return remote(ext4.at[own_rows(d), mid_cols], ext4.at[halo_rows(d), mid_cols],
                      t_send.at[d], t_recv.at[d], s_to(d))

    def corner1(d, e):
        i = 2 * e + d
        return remote(ext4.at[own_rows(d), side_cols[e]], ext4.at[halo_rows(d), side_cols[e]],
                      q_send.at[i], q_recv.at[i], s_to(d))

    def far_rows(d):
        return pl.ds(d * (R + W), W)

    def corner2(d, e):
        i = 2 * e + d
        return remote(fix4.at[far_rows(d), side_cols[e]], rs.at[pl.ds(W * (1 - d), W), side_cols[e]],
                      b_send.at[i], b_recv.at[i], s_to(d))

    def stream2(d):
        return remote(fix4.at[far_rows(d), mid_cols], rs.at[pl.ds(W * (1 - d), W), mid_cols],
                      d_send.at[d], d_recv.at[d], s_to(d))

    def cross2(e, d):
        i = 2 * e + d
        return remote(msum.at[pl.ds(W * d, W), pl.ds(W * e, W)],
                      rc.at[pl.ds(W * d, W), pl.ds(W * (1 - e), W)],
                      m_send.at[i], m_recv.at[i], c_to(e))

    def when(cond, run):
        pl.when(cond)(run)

    pl.semaphore_wait(barrier, ns - 1 + c_has(0).astype(jnp.int32) + c_has(1).astype(jnp.int32))

    for d in (far, near):
        for e in range(2):
            when(c_has(e), lambda: cross1(e, d).start())
    mask(range(W, C - W))
    for d in (far, near):
        when(s_has(d), lambda: stream1(d).start())

    def sums(i, carry):
        for j in range(0, C, 2):
            rows = []
            for u in range(2):
                block = ext4[i + W, j + W + u].astype(f32)
                rows.append(block.reshape(4, width // 4, sides).sum(axis=1))
            first = pl.multiple_of((i * C + j) * 4, 8)
            pb[pl.ds(first, 8), :] = jnp.concatenate(rows, axis=0)
        return carry

    lax.fori_loop(0, R, sums, 0)
    loads[1].wait()
    n_own = R * C
    lane = lax.broadcasted_iota(jnp.int32, (8, 4 * n_own), 1)
    key = jnp.zeros((8, 4 * n_own), jnp.int32)
    for i in range(R):
        for j in range(C):
            key = jnp.where(lane // 4 == i * C + j, aggregate[i, j], key)
    key = (key * 4 + lane % 4)[0:1]
    row = lax.broadcasted_iota(jnp.int32, (4 * owned * ns, 4 * n_own), 0)
    chosen = (row == jnp.broadcast_to(key, row.shape)).astype(f32)
    restricted = jnp.dot(chosen, pb[...], precision=lax.Precision.HIGHEST,
                         preferred_element_type=f32)
    for o in range(ns):
        partial[o] = restricted[o * 4 * owned:(o + 1) * 4 * owned]

    def give(k):
        to = lax.rem(s + k, ns)
        return remote(partial.at[to], part_in.at[k - 1], p_send.at[k - 1], p_recv.at[k - 1],
                      {"stream": to})

    def share(k, mine):
        part = coarse_all.at[pl.ds(mine * owned, owned)]
        return remote(part, part, g_send.at[k - 1], g_recv.at[k - 1],
                      {"stream": lax.rem(s + k, ns)})

    for k in range(1, ns):
        give(k).start()

    for d in (far, near):
        for e in range(2):
            @pl.when(c_has(1 - e))
            def _():
                cross1(e, d).wait_recv()
                when(s_has(d), lambda: corner1(d, 1 - e).start())

    loads[3].wait()
    loads[4].wait()
    for d in range(2):
        when(s_has(1 - d), lambda: stream1(d).wait_recv())
    for d in (near, far):
        for e in range(2):
            when(s_has(1 - d) & c_has(e), lambda: corner1(d, e).wait_recv())

    ext = ext4.reshape(RE * CE, width, sides)

    def fix_of(i, j):
        n = i * CE + j
        picked = jnp.concatenate(
            [ext[pattern[0, k, n]] for k in range(a_mat.shape[2] // width)], axis=0)
        return jnp.dot(a_mat[n], picked, preferred_element_type=f32)

    edge = tuple(range(W)) + tuple(range(C + W, CE))
    middle = tuple(range(W, C + W))

    def put(i, cols):
        for j in cols:
            fix4[i, j] = fix_of(i, j).astype(bf16)

    def fold(d):
        for e in range(2):
            @pl.when(c_has(e))
            def _():
                when(s_has(d), lambda: corner2(1 - d, e).wait_recv())
                for t in range(W):
                    i = W * d + t
                    for j in range(W):
                        col = e * (C + W) + j
                        msum[i, e * W + j] = (
                            fix4[i + W, col].astype(f32) + rs[i, col].astype(f32)).astype(bf16)
                cross2(e, d).start()

    def coarse_step():
        loads[2].wait()
        total = partial[s]
        for k in range(1, ns):
            give(k).wait_recv()
            total = total + part_in[k - 1]
        coarse = jnp.dot(coarse_inv[...], total, precision=lax.Precision.HIGHEST,
                         preferred_element_type=f32)
        for a in range(owned):
            coarse_all[s * owned + a] = coarse[4 * a:4 * a + 4]
        for k in range(1, ns):
            share(k, s).start()

    def edges(p, carry):
        d = lax.rem(p, 2) * far + (1 - lax.rem(p, 2)) * near
        first = jnp.where(p < 2, d * (R + W), W + W * d)
        for u in range(W):
            put(first + u, edge)

        @pl.when(p < 2)
        def _():
            for e in range(2):
                when(s_has(d) & c_has(e), lambda: corner2(d, e).start())

        @pl.when(p == 2)
        def _():
            fold(near)
            coarse_step()

        return carry

    lax.fori_loop(0, 4, edges, 0)

    def rows(p, carry):
        q = p // W
        d = jnp.where(q == 0, far, near)
        put(jnp.where(q < 2, d * (R + W) + lax.rem(p, W), p - W), middle)

        @pl.when((lax.rem(p, W) == W - 1) & (q < 2))
        def _():
            when(s_has(d), lambda: stream2(d).start())
            when(q == 0, lambda: fold(far))

        return carry

    lax.fori_loop(0, 2 * W + R, rows, 0)

    for k in range(1, ns):
        share(k, lax.rem(s + ns - k, ns)).wait_recv()

    for d in range(2):
        when(s_has(1 - d), lambda: stream2(d).wait_recv())

    def kept(i, j, value):
        keep = jnp.full(value.shape, i * C + j, jnp.int32) < live
        return jnp.where(keep, value, 0.0)

    def add_stream(i, carry):
        for j in range(C):
            values = coarse_all[aggregate[i, j]]
            spread = jnp.concatenate(
                [jnp.broadcast_to(values[f:f + 1], (width // 4, sides)) for f in range(4)], axis=0)
            fine = fix4[i + W, j + W].astype(f32) + rs[i, j + W].astype(f32)
            out[i, j] = kept(i, j, fine + spread)
        return carry

    lax.fori_loop(0, R, add_stream, 0)

    def add_cross(d):
        for e in range(2):
            when(c_has(1 - e), lambda: cross2(e, d).wait_recv())
        for t in range(W):
            i = W * d + t
            for j in range(W):
                for col, at in ((j, j), (C - W + j, W + j)):
                    out[i, col] = kept(i, col, out[i, col] + rc[i, at].astype(f32))

    add_cross(near)
    add_cross(far)

    for e in range(2):
        @pl.when(c_has(e))
        def _():
            for d in range(2):
                cross1(e, d).wait_send()
                cross2(e, d).wait_send()
    for d in range(2):
        @pl.when(s_has(d))
        def _():
            stream1(d).wait_send()
            stream2(d).wait_send()
            for e in range(2):
                @pl.when(c_has(e))
                def _():
                    corner1(d, e).wait_send()
                    corner2(d, e).wait_send()
    for k in range(1, ns):
        give(k).wait_send()
        share(k, s).wait_send()


def body(ns, nc, residual, approx_inverse, pattern, live_blocks, block_aggregate, coarse_inverse):
    R, C, width, sides = residual.shape
    _, extent, _, depth = approx_inverse.shape
    owned = coarse_inverse.shape[0] // 4
    bf16, f32, i32 = jnp.bfloat16, jnp.float32, jnp.int32
    dma = pltpu.SemaphoreType.DMA
    hbm = pl.BlockSpec(memory_space=pltpu.HBM)
    vmem = pl.BlockSpec(memory_space=pltpu.VMEM)
    RE, CE = R + 2 * W, C + 2 * W
    links = jnp.transpose(pattern, (0, 2, 1))
    operands = (residual, approx_inverse, links, block_aggregate, coarse_inverse)
    return pl.pallas_call(
        functools.partial(kernel, ns, nc, R, C),
        out_shape=pltpu.VMEM(residual.shape, f32),
        in_specs=[pl.BlockSpec(memory_space=pltpu.SMEM)] + [hbm] * 5,
        out_specs=vmem,
        scratch_shapes=[
            pltpu.VMEM(residual.shape, bf16),
            pltpu.VMEM((extent, width, depth), bf16),
            pltpu.SMEM(links.shape, i32),
            pltpu.SMEM(block_aggregate.shape, i32),
            pltpu.VMEM(coarse_inverse.shape, f32),
            pltpu.VMEM((RE, CE, width, sides), bf16),
            pltpu.VMEM((RE, CE, width, sides), bf16),
            pltpu.VMEM((2 * W, CE, width, sides), bf16),
            pltpu.VMEM((R, 2 * W, width, sides), bf16),
            pltpu.VMEM((R, 2 * W, width, sides), bf16),
            pltpu.VMEM((R * C * 4, sides), f32),
            pltpu.VMEM((ns, 4 * owned, sides), f32),
            pltpu.VMEM((ns - 1, 4 * owned, sides), f32),
            pltpu.VMEM((ns * owned, 4, sides), f32),
            dma((5,)),
            dma((4,)), dma((4,)), dma((2,)), dma((2,)), dma((4,)), dma((4,)),
            dma((ns - 1,)), dma((ns - 1,)), dma((ns - 1,)), dma((ns - 1,)),
            dma((4,)), dma((4,)), dma((2,)), dma((2,)), dma((4,)), dma((4,)),
        ],
        compiler_params=pltpu.CompilerParams(
            collective_id=0, has_side_effects=True, vmem_limit_bytes=40 * 1024 * 1024),
        cost_estimate=pl.CostEstimate(
            flops=2 * extent * width * depth * sides,
            bytes_accessed=extent * width * depth * 2 + residual.size * 6,
            transcendentals=0),
    )(live_blocks, *(pltpu.with_memory_space_constraint(array, pltpu.HBM) for array in operands))


def solution(mesh):
    placed = (
        P("stream", "cross", None, None),
        P("stream", "cross", None, None),
        P("stream", "cross", None),
        P("stream", "cross"),
        P("stream", "cross"),
        P("stream", "cross"),
    )
    return jax.shard_map(
        functools.partial(body, mesh.shape["stream"], mesh.shape["cross"]),
        mesh=mesh,
        in_specs=placed,
        out_specs=P("stream", "cross", None, None),
        check_vma=False,
    )
```

```python
import functools

import jax
import jax.numpy as jnp
from jax import lax
from jax.experimental import pallas as pl
from jax.experimental.pallas import tpu as pltpu
from jax.sharding import PartitionSpec as P

W = 2


def kernel(
    ns, nc, R, C,
    live_ref, residual, inverse, pattern_in, aggregate_in, coarse_in,
    out,
    res, a_mat, pattern, aggregate, coarse_inv,
    ext4, fix4, rs, rc, msum, pb, partial, part_in, coarse_all,
    in_sem, h_send, h_recv, t_send, t_recv, q_send, q_recv, p_send, p_recv, g_send, g_recv,
    b_send, b_recv, d_send, d_recv, m_send, m_recv,
):
    s = lax.axis_index("stream")
    c = lax.axis_index("cross")
    width, sides = res.shape[2], res.shape[3]
    CE = C + 2 * W
    RE = R + 2 * W
    owned = coarse_inv.shape[0] // 4
    bf16, f32 = jnp.bfloat16, jnp.float32

    far = lax.rem(s, 2)
    near = 1 - far
    long = lax.rem(c, 2)
    short = 1 - long

    def s_has(d):
        to = s + 2 * d - 1
        return (to >= 0) & (to < ns)

    def c_has(e):
        to = c + 2 * e - 1
        return (to >= 0) & (to < nc)

    def s_to(d):
        return {"stream": jnp.clip(s + 2 * d - 1, 0, ns - 1)}

    def c_to(e):
        return {"cross": jnp.clip(c + 2 * e - 1, 0, nc - 1)}

    loads = [
        pltpu.make_async_copy(residual, res, in_sem.at[0]),
        pltpu.make_async_copy(aggregate_in, aggregate, in_sem.at[1]),
        pltpu.make_async_copy(coarse_in, coarse_inv, in_sem.at[2]),
        pltpu.make_async_copy(pattern_in, pattern, in_sem.at[3]),
        pltpu.make_async_copy(inverse.at[0], a_mat, in_sem.at[4]),
    ]
    for load in loads:
        load.start()

    barrier = pltpu.get_barrier_semaphore()
    for e in range(2):
        @pl.when(c_has(e))
        def _():
            pl.semaphore_signal(barrier, inc=1, device_id=c_to(e),
                                device_id_type=pl.DeviceIdType.MESH)
    for k in range(1, ns):
        pl.semaphore_signal(barrier, inc=1, device_id={"stream": lax.rem(s + k, ns)},
                            device_id_type=pl.DeviceIdType.MESH)

    def zero(ref, rows, cols):
        ref[rows[0]:rows[1], cols[0]:cols[1]] = jnp.zeros(
            (rows[1] - rows[0], cols[1] - cols[0], width, sides), bf16)

    @pl.when(s == 0)
    def _():
        zero(ext4, (0, W), (0, CE))
        zero(rs, (0, W), (0, CE))

    @pl.when(s == ns - 1)
    def _():
        zero(ext4, (R + W, RE), (0, CE))
        zero(rs, (W, 2 * W), (0, CE))

    @pl.when(c == 0)
    def _():
        zero(ext4, (0, RE), (0, W))
        zero(rc, (0, R), (0, W))

    @pl.when(c == nc - 1)
    def _():
        zero(ext4, (0, RE), (C + W, CE))
        zero(rc, (0, R), (W, 2 * W))

    live = live_ref[0, 0]
    loads[0].wait()

    def mask(cols):
        def row(i, carry):
            for j in cols:
                block = res[i, j]
                keep = jnp.full(block.shape, i * C + j, jnp.int32) < live
                ext4[i + W, j + W] = jnp.where(keep, block.astype(f32), 0.0).astype(bf16)
            return carry

        lax.fori_loop(0, R, row, 0)

    mask(tuple(range(W)) + tuple(range(C - W, C)))

    def own_cols(e):
        return pl.ds(W + e * (C - W), W)

    def halo_cols(e):
        return pl.ds((1 - e) * (C + W), W)

    def side_cols(e):
        return pl.ds(e * (C + W), W)

    mid_cols = pl.ds(W, C)

    def remote(src, dst, send, recv, to):
        return pltpu.make_async_remote_copy(
            src_ref=src, dst_ref=dst, send_sem=send, recv_sem=recv,
            device_id=to, device_id_type=pl.DeviceIdType.MESH)

    def own_rows(d):
        return pl.ds(W + W * d, W)

    def halo_rows(d):
        return pl.ds((1 - d) * (R + W), W)

    def cross1(e, d):
        i = 2 * e + d
        return remote(ext4.at[own_rows(d), own_cols(e)], ext4.at[own_rows(d), halo_cols(e)],
                      h_send.at[i], h_recv.at[i], c_to(e))

    def stream1(d):
        return remote(ext4.at[own_rows(d), mid_cols], ext4.at[halo_rows(d), mid_cols],
                      t_send.at[d], t_recv.at[d], s_to(d))

    def corner1(d, e):
        i = 2 * e + d
        return remote(ext4.at[own_rows(d), side_cols(e)], ext4.at[halo_rows(d), side_cols(e)],
                      q_send.at[i], q_recv.at[i], s_to(d))

    def far_rows(d):
        return pl.ds(d * (R + W), W)

    def corner2(d, e):
        i = 2 * e + d
        return remote(fix4.at[far_rows(d), side_cols(e)], rs.at[pl.ds(W * (1 - d), W), side_cols(e)],
                      b_send.at[i], b_recv.at[i], s_to(d))

    def stream2(d):
        return remote(fix4.at[far_rows(d), mid_cols], rs.at[pl.ds(W * (1 - d), W), mid_cols],
                      d_send.at[d], d_recv.at[d], s_to(d))

    def cross2(e, d):
        i = 2 * e + d
        return remote(msum.at[pl.ds(W * d, W), pl.ds(W * e, W)],
                      rc.at[pl.ds(W * d, W), pl.ds(W * (1 - e), W)],
                      m_send.at[i], m_recv.at[i], c_to(e))

    def when(cond, run):
        pl.when(cond)(run)

    pl.semaphore_wait(barrier, ns - 1 + c_has(0).astype(jnp.int32) + c_has(1).astype(jnp.int32))

    for d in (far, near):
        for e in (long, short):
            when(c_has(e), lambda: cross1(e, d).start())
    mask(range(W, C - W))
    for d in (far, near):
        when(s_has(d), lambda: stream1(d).start())

    def forward(d):
        for e in (short, long):
            @pl.when(c_has(1 - e))
            def _():
                cross1(e, d).wait_recv()
                when(s_has(d), lambda: corner1(d, 1 - e).start())

    forward(far)

    def sums(i, carry):
        for j in range(0, C, 2):
            rows = []
            for u in range(2):
                block = ext4[i + W, j + W + u].astype(f32)
                rows.append(block.reshape(4, width // 4, sides).sum(axis=1))
            first = pl.multiple_of((i * C + j) * 4, 8)
            pb[pl.ds(first, 8), :] = jnp.concatenate(rows, axis=0)
        return carry

    lax.fori_loop(0, R, sums, 0)
    loads[1].wait()
    n_own = R * C
    lane = lax.broadcasted_iota(jnp.int32, (8, 4 * n_own), 1)
    key = jnp.zeros((8, 4 * n_own), jnp.int32)
    for i in range(R):
        for j in range(C):
            key = jnp.where(lane // 4 == i * C + j, aggregate[i, j], key)
    key = (key * 4 + lane % 4)[0:1]
    row = lax.broadcasted_iota(jnp.int32, (4 * owned * ns, 4 * n_own), 0)
    chosen = (row == jnp.broadcast_to(key, row.shape)).astype(f32)
    restricted = jnp.dot(chosen, pb[...], precision=lax.Precision.HIGHEST,
                         preferred_element_type=f32)
    for o in range(ns):
        partial[o] = restricted[o * 4 * owned:(o + 1) * 4 * owned]

    def give(k):
        to = lax.rem(s + k, ns)
        return remote(partial.at[to], part_in.at[k - 1], p_send.at[k - 1], p_recv.at[k - 1],
                      {"stream": to})

    def share(k, mine):
        part = coarse_all.at[pl.ds(mine * owned, owned)]
        return remote(part, part, g_send.at[k - 1], g_recv.at[k - 1],
                      {"stream": lax.rem(s + k, ns)})

    for k in range(1, ns):
        give(k).start()

    forward(near)

    loads[3].wait()
    loads[4].wait()
    for d in range(2):
        when(s_has(1 - d), lambda: stream1(d).wait_recv())
    for d in (near, far):
        for e in range(2):
            when(s_has(1 - d) & c_has(e), lambda: corner1(d, e).wait_recv())

    ext = ext4.reshape(RE * CE, width, sides)

    def fix_of(i, j):
        n = i * CE + j
        picked = jnp.concatenate(
            [ext[pattern[0, k, n]] for k in range(a_mat.shape[2] // width)], axis=0)
        return jnp.dot(a_mat[n], picked, preferred_element_type=f32)

    edge = tuple(range(W)) + tuple(range(C + W, CE))
    middle = tuple(range(W, C + W))

    def put(i, cols):
        for j in cols:
            fix4[i, j] = fix_of(i, j).astype(bf16)

    def fold(d):
        for e in (long, short):
            @pl.when(c_has(e))
            def _():
                when(s_has(d), lambda: corner2(1 - d, e).wait_recv())
                for t in range(W):
                    i = W * d + t
                    for j in range(W):
                        col = e * (C + W) + j
                        msum[i, e * W + j] = (
                            fix4[i + W, col].astype(f32) + rs[i, col].astype(f32)).astype(bf16)
                cross2(e, d).start()

    def coarse_step():
        loads[2].wait()
        total = partial[s]
        for k in range(1, ns):
            give(k).wait_recv()
            total = total + part_in[k - 1]
        coarse = jnp.dot(coarse_inv[...], total, precision=lax.Precision.HIGHEST,
                         preferred_element_type=f32)
        for a in range(owned):
            coarse_all[s * owned + a] = coarse[4 * a:4 * a + 4]
        for k in range(1, ns):
            share(k, s).start()

    def sweep(first, count, cols):
        def row(u, carry):
            put(first + u, cols)
            return carry

        lax.fori_loop(0, count, row, 0)

    def edges(p, carry):
        d = jnp.where(p == 0, near, far)
        for u in range(W):
            put(d * (R + W) + u, edge)
        for e in range(2):
            when(s_has(d) & c_has(e), lambda: corner2(d, e).start())
        return carry

    lax.fori_loop(0, 2, edges, 0)
    sweep(W + W * near, W, edge)
    fold(near)
    sweep(far * (R + W), W, middle)
    when(s_has(far), lambda: stream2(far).start())
    sweep(W + W * far, W, edge)
    fold(far)
    coarse_step()
    sweep(near * (R + W), W, middle)
    when(s_has(near), lambda: stream2(near).start())
    sweep(W, R, middle)

    for k in range(1, ns):
        share(k, lax.rem(s + ns - k, ns)).wait_recv()

    def kept(i, j, value):
        keep = jnp.full(value.shape, i * C + j, jnp.int32) < live
        return jnp.where(keep, value, 0.0)

    def finish(d):
        when(s_has(d), lambda: stream2(1 - d).wait_recv())

        def add_stream(u, carry):
            i = W * d + u
            for j in range(C):
                values = coarse_all[aggregate[i, j]]
                spread = jnp.concatenate(
                    [jnp.broadcast_to(values[f:f + 1], (width // 4, sides)) for f in range(4)],
                    axis=0)
                fine = fix4[i + W, j + W].astype(f32) + rs[i, j + W].astype(f32)
                out[i, j] = kept(i, j, fine + spread)
            return carry

        lax.fori_loop(0, W, add_stream, 0)
        for e in (short, long):
            when(c_has(1 - e), lambda: cross2(e, d).wait_recv())
        for u in range(W):
            i = W * d + u
            for j in range(W):
                for col, at in ((j, j), (C - W + j, W + j)):
                    out[i, col] = kept(i, col, out[i, col] + rc[i, at].astype(f32))

    finish(near)
    finish(far)

    for e in range(2):
        @pl.when(c_has(e))
        def _():
            for d in range(2):
                cross1(e, d).wait_send()
                cross2(e, d).wait_send()
    for d in range(2):
        @pl.when(s_has(d))
        def _():
            stream1(d).wait_send()
            stream2(d).wait_send()
            for e in range(2):
                @pl.when(c_has(e))
                def _():
                    corner1(d, e).wait_send()
                    corner2(d, e).wait_send()
    for k in range(1, ns):
        give(k).wait_send()
        share(k, s).wait_send()


def body(ns, nc, residual, approx_inverse, pattern, live_blocks, block_aggregate, coarse_inverse):
    R, C, width, sides = residual.shape
    _, extent, _, depth = approx_inverse.shape
    owned = coarse_inverse.shape[0] // 4
    bf16, f32, i32 = jnp.bfloat16, jnp.float32, jnp.int32
    dma = pltpu.SemaphoreType.DMA
    hbm = pl.BlockSpec(memory_space=pltpu.HBM)
    vmem = pl.BlockSpec(memory_space=pltpu.VMEM)
    RE, CE = R + 2 * W, C + 2 * W
    links = jnp.transpose(pattern, (0, 2, 1))
    operands = (residual, approx_inverse, links, block_aggregate, coarse_inverse)
    return pl.pallas_call(
        functools.partial(kernel, ns, nc, R, C),
        out_shape=pltpu.VMEM(residual.shape, f32),
        in_specs=[pl.BlockSpec(memory_space=pltpu.SMEM)] + [hbm] * 5,
        out_specs=vmem,
        scratch_shapes=[
            pltpu.VMEM(residual.shape, bf16),
            pltpu.VMEM((extent, width, depth), bf16),
            pltpu.SMEM(links.shape, i32),
            pltpu.SMEM(block_aggregate.shape, i32),
            pltpu.VMEM(coarse_inverse.shape, f32),
            pltpu.VMEM((RE, CE, width, sides), bf16),
            pltpu.VMEM((RE, CE, width, sides), bf16),
            pltpu.VMEM((2 * W, CE, width, sides), bf16),
            pltpu.VMEM((R, 2 * W, width, sides), bf16),
            pltpu.VMEM((R, 2 * W, width, sides), bf16),
            pltpu.VMEM((R * C * 4, sides), f32),
            pltpu.VMEM((ns, 4 * owned, sides), f32),
            pltpu.VMEM((ns - 1, 4 * owned, sides), f32),
            pltpu.VMEM((ns * owned, 4, sides), f32),
            dma((5,)),
            dma((4,)), dma((4,)), dma((2,)), dma((2,)), dma((4,)), dma((4,)),
            dma((ns - 1,)), dma((ns - 1,)), dma((ns - 1,)), dma((ns - 1,)),
            dma((4,)), dma((4,)), dma((2,)), dma((2,)), dma((4,)), dma((4,)),
        ],
        compiler_params=pltpu.CompilerParams(
            collective_id=0, has_side_effects=True, vmem_limit_bytes=40 * 1024 * 1024),
        cost_estimate=pl.CostEstimate(
            flops=2 * extent * width * depth * sides,
            bytes_accessed=extent * width * depth * 2 + residual.size * 6,
            transcendentals=0),
    )(live_blocks, *(pltpu.with_memory_space_constraint(array, pltpu.HBM) for array in operands))


def solution(mesh):
    placed = (
        P("stream", "cross", None, None),
        P("stream", "cross", None, None),
        P("stream", "cross", None),
        P("stream", "cross"),
        P("stream", "cross"),
        P("stream", "cross"),
    )
    return jax.shard_map(
        functools.partial(body, mesh.shape["stream"], mesh.shape["cross"]),
        mesh=mesh,
        in_specs=placed,
        out_specs=P("stream", "cross", None, None),
        check_vma=False,
    )
```

```python
import functools

import jax
import jax.numpy as jnp
from jax import lax
from jax.experimental import pallas as pl
from jax.experimental.pallas import tpu as pltpu
from jax.sharding import PartitionSpec as P

W = 2


def kernel(
    ns, nc, R, C,
    live_ref, residual, inverse, pattern_in, aggregate_in, coarse_in,
    out,
    res, a_mat, pattern, aggregate, coarse_inv,
    ext4, fix4, rs, rc, msum, pb, partial, part_in, coarse_all,
    in_sem, h_send, h_recv, t_send, t_recv, q_send, q_recv, p_send, p_recv, g_send, g_recv,
    b_send, b_recv, d_send, d_recv, m_send, m_recv,
):
    s = lax.axis_index("stream")
    c = lax.axis_index("cross")
    width, sides = res.shape[2], res.shape[3]
    CE = C + 2 * W
    RE = R + 2 * W
    owned = coarse_inv.shape[0] // 4
    bf16, f32 = jnp.bfloat16, jnp.float32

    far = lax.rem(s, 2)
    near = 1 - far
    long = lax.rem(c, 2)
    short = 1 - long

    def s_has(d):
        to = s + 2 * d - 1
        return (to >= 0) & (to < ns)

    def c_has(e):
        to = c + 2 * e - 1
        return (to >= 0) & (to < nc)

    def s_to(d):
        return {"stream": jnp.clip(s + 2 * d - 1, 0, ns - 1)}

    def c_to(e):
        return {"cross": jnp.clip(c + 2 * e - 1, 0, nc - 1)}

    loads = [
        pltpu.make_async_copy(residual, res, in_sem.at[0]),
        pltpu.make_async_copy(aggregate_in, aggregate, in_sem.at[1]),
        pltpu.make_async_copy(coarse_in, coarse_inv, in_sem.at[2]),
        pltpu.make_async_copy(pattern_in, pattern, in_sem.at[3]),
        pltpu.make_async_copy(inverse.at[0], a_mat, in_sem.at[4]),
    ]
    loads[0].start()

    barrier = pltpu.get_barrier_semaphore()
    for e in range(2):
        @pl.when(c_has(e))
        def _():
            pl.semaphore_signal(barrier, inc=1, device_id=c_to(e),
                                device_id_type=pl.DeviceIdType.MESH)
    for k in range(1, ns):
        pl.semaphore_signal(barrier, inc=1, device_id={"stream": lax.rem(s + k, ns)},
                            device_id_type=pl.DeviceIdType.MESH)

    for load in loads[1:]:
        load.start()

    def zero(ref, rows, cols):
        ref[rows[0]:rows[1], cols[0]:cols[1]] = jnp.zeros(
            (rows[1] - rows[0], cols[1] - cols[0], width, sides), bf16)

    @pl.when(s == 0)
    def _():
        zero(ext4, (0, W), (0, CE))
        zero(rs, (0, W), (0, CE))

    @pl.when(s == ns - 1)
    def _():
        zero(ext4, (R + W, RE), (0, CE))
        zero(rs, (W, 2 * W), (0, CE))

    @pl.when(c == 0)
    def _():
        zero(ext4, (0, RE), (0, W))
        zero(rc, (0, R), (0, W))

    @pl.when(c == nc - 1)
    def _():
        zero(ext4, (0, RE), (C + W, CE))
        zero(rc, (0, R), (W, 2 * W))

    live = live_ref[0, 0]
    loads[0].wait()

    def mask(cols):
        def row(i, carry):
            for j in cols:
                block = res[i, j]
                keep = jnp.full(block.shape, i * C + j, jnp.int32) < live
                ext4[i + W, j + W] = jnp.where(keep, block.astype(f32), 0.0).astype(bf16)
            return carry

        lax.fori_loop(0, R, row, 0)

    mask(tuple(range(W)) + tuple(range(C - W, C)))

    def own_cols(e):
        return pl.ds(W + e * (C - W), W)

    def halo_cols(e):
        return pl.ds((1 - e) * (C + W), W)

    def side_cols(e):
        return pl.ds(e * (C + W), W)

    mid_cols = pl.ds(W, C)

    def remote(src, dst, send, recv, to):
        return pltpu.make_async_remote_copy(
            src_ref=src, dst_ref=dst, send_sem=send, recv_sem=recv,
            device_id=to, device_id_type=pl.DeviceIdType.MESH)

    def own_rows(d):
        return pl.ds(W + W * d, W)

    def halo_rows(d):
        return pl.ds((1 - d) * (R + W), W)

    def cross1(e, d):
        i = 2 * e + d
        return remote(ext4.at[own_rows(d), own_cols(e)], ext4.at[own_rows(d), halo_cols(e)],
                      h_send.at[i], h_recv.at[i], c_to(e))

    def stream1(d):
        return remote(ext4.at[own_rows(d), mid_cols], ext4.at[halo_rows(d), mid_cols],
                      t_send.at[d], t_recv.at[d], s_to(d))

    def corner1(d, e):
        i = 2 * e + d
        return remote(ext4.at[own_rows(d), side_cols(e)], ext4.at[halo_rows(d), side_cols(e)],
                      q_send.at[i], q_recv.at[i], s_to(d))

    def far_rows(d):
        return pl.ds(d * (R + W), W)

    def corner2(d, e):
        i = 2 * e + d
        return remote(fix4.at[far_rows(d), side_cols(e)], rs.at[pl.ds(W * (1 - d), W), side_cols(e)],
                      b_send.at[i], b_recv.at[i], s_to(d))

    def stream2(d):
        return remote(fix4.at[far_rows(d), mid_cols], rs.at[pl.ds(W * (1 - d), W), mid_cols],
                      d_send.at[d], d_recv.at[d], s_to(d))

    def cross2(e, d):
        i = 2 * e + d
        return remote(msum.at[pl.ds(W * d, W), pl.ds(W * e, W)],
                      rc.at[pl.ds(W * d, W), pl.ds(W * (1 - e), W)],
                      m_send.at[i], m_recv.at[i], c_to(e))

    def when(cond, run):
        pl.when(cond)(run)

    pl.semaphore_wait(barrier, ns - 1 + c_has(0).astype(jnp.int32) + c_has(1).astype(jnp.int32))

    for d in (far, near):
        for e in (long, short):
            when(c_has(e), lambda: cross1(e, d).start())
    mask(range(W, C - W))
    for d in (far, near):
        when(s_has(d), lambda: stream1(d).start())

    def forward(d):
        for e in (short, long):
            @pl.when(c_has(1 - e))
            def _():
                cross1(e, d).wait_recv()
                when(s_has(d), lambda: corner1(d, 1 - e).start())

    forward(far)

    def sums(i, carry):
        for j in range(0, C, 2):
            rows = []
            for u in range(2):
                block = ext4[i + W, j + W + u].astype(f32)
                rows.append(block.reshape(4, width // 4, sides).sum(axis=1))
            first = pl.multiple_of((i * C + j) * 4, 8)
            pb[pl.ds(first, 8), :] = jnp.concatenate(rows, axis=0)
        return carry

    lax.fori_loop(0, R, sums, 0)
    loads[1].wait()
    n_own = R * C
    lane = lax.broadcasted_iota(jnp.int32, (8, 4 * n_own), 1)
    key = jnp.zeros((8, 4 * n_own), jnp.int32)
    for i in range(R):
        for j in range(C):
            key = jnp.where(lane // 4 == i * C + j, aggregate[i, j], key)
    key = (key * 4 + lane % 4)[0:1]
    row = lax.broadcasted_iota(jnp.int32, (4 * owned * ns, 4 * n_own), 0)
    chosen = (row == jnp.broadcast_to(key, row.shape)).astype(f32)
    restricted = jnp.dot(chosen, pb[...], precision=lax.Precision.HIGHEST,
                         preferred_element_type=f32)
    for o in range(ns):
        partial[o] = restricted[o * 4 * owned:(o + 1) * 4 * owned]

    def give(k):
        to = lax.rem(s + k, ns)
        return remote(partial.at[to], part_in.at[k - 1], p_send.at[k - 1], p_recv.at[k - 1],
                      {"stream": to})

    def share(k, mine):
        part = coarse_all.at[pl.ds(mine * owned, owned)]
        return remote(part, part, g_send.at[k - 1], g_recv.at[k - 1],
                      {"stream": lax.rem(s + k, ns)})

    for k in range(1, ns):
        give(k).start()

    forward(near)

    loads[3].wait()
    loads[4].wait()
    for d in range(2):
        when(s_has(1 - d), lambda: stream1(d).wait_recv())
    for d in (near, far):
        for e in range(2):
            when(s_has(1 - d) & c_has(e), lambda: corner1(d, e).wait_recv())

    ext = ext4.reshape(RE * CE, width, sides)

    def fix_of(i, j):
        n = i * CE + j
        picked = jnp.concatenate(
            [ext[pattern[0, k, n]] for k in range(a_mat.shape[2] // width)], axis=0)
        return jnp.dot(a_mat[n], picked, preferred_element_type=f32)

    edge = tuple(range(W)) + tuple(range(C + W, CE))
    middle = tuple(range(W, C + W))

    def put(i, cols):
        for j in cols:
            fix4[i, j] = fix_of(i, j).astype(bf16)

    def fold(d):
        for e in (long, short):
            @pl.when(c_has(e))
            def _():
                when(s_has(d), lambda: corner2(1 - d, e).wait_recv())
                for t in range(W):
                    i = W * d + t
                    for j in range(W):
                        col = e * (C + W) + j
                        msum[i, e * W + j] = (
                            fix4[i + W, col].astype(f32) + rs[i, col].astype(f32)).astype(bf16)
                cross2(e, d).start()

    def coarse_step():
        loads[2].wait()
        total = partial[s]
        for k in range(1, ns):
            give(k).wait_recv()
            total = total + part_in[k - 1]
        coarse = jnp.dot(coarse_inv[...], total, precision=lax.Precision.HIGHEST,
                         preferred_element_type=f32)
        for a in range(owned):
            coarse_all[s * owned + a] = coarse[4 * a:4 * a + 4]
        for k in range(1, ns):
            share(k, s).start()

    def sweep(first, count, cols):
        def row(u, carry):
            put(first + u, cols)
            return carry

        lax.fori_loop(0, count, row, 0)

    def margin(d):
        for u in range(W):
            put(d * (R + W) + u, edge)
        for e in (long, short):
            when(s_has(d) & c_has(e), lambda: corner2(d, e).start())

    def own_edges(d):
        for u in range(W):
            put(W + W * d + u, edge)

    margin(near)
    own_edges(near)
    margin(far)
    fold(near)
    sweep(far * (R + W), W, middle)
    when(s_has(far), lambda: stream2(far).start())
    own_edges(far)
    fold(far)
    coarse_step()
    sweep(near * (R + W), W, middle)
    when(s_has(near), lambda: stream2(near).start())
    sweep(W, R, middle)

    for k in range(1, ns):
        share(k, lax.rem(s + ns - k, ns)).wait_recv()

    def kept(i, j, value):
        keep = jnp.full(value.shape, i * C + j, jnp.int32) < live
        return jnp.where(keep, value, 0.0)

    def finish(d):
        when(s_has(d), lambda: stream2(1 - d).wait_recv())

        def add_stream(u, carry):
            i = W * d + u
            for j in range(C):
                values = coarse_all[aggregate[i, j]]
                spread = jnp.concatenate(
                    [jnp.broadcast_to(values[f:f + 1], (width // 4, sides)) for f in range(4)],
                    axis=0)
                fine = fix4[i + W, j + W].astype(f32) + rs[i, j + W].astype(f32)
                out[i, j] = kept(i, j, fine + spread)
            return carry

        lax.fori_loop(0, W, add_stream, 0)
        for e in (short, long):
            when(c_has(1 - e), lambda: cross2(e, d).wait_recv())
        for u in range(W):
            i = W * d + u
            for j in range(W):
                for col, at in ((j, j), (C - W + j, W + j)):
                    out[i, col] = kept(i, col, out[i, col] + rc[i, at].astype(f32))

    finish(near)
    finish(far)

    for e in range(2):
        @pl.when(c_has(e))
        def _():
            for d in range(2):
                cross1(e, d).wait_send()
                cross2(e, d).wait_send()
    for d in range(2):
        @pl.when(s_has(d))
        def _():
            stream1(d).wait_send()
            stream2(d).wait_send()
            for e in range(2):
                @pl.when(c_has(e))
                def _():
                    corner1(d, e).wait_send()
                    corner2(d, e).wait_send()
    for k in range(1, ns):
        give(k).wait_send()
        share(k, s).wait_send()


def body(ns, nc, residual, approx_inverse, pattern, live_blocks, block_aggregate, coarse_inverse):
    R, C, width, sides = residual.shape
    _, extent, _, depth = approx_inverse.shape
    owned = coarse_inverse.shape[0] // 4
    bf16, f32, i32 = jnp.bfloat16, jnp.float32, jnp.int32
    dma = pltpu.SemaphoreType.DMA
    hbm = pl.BlockSpec(memory_space=pltpu.HBM)
    vmem = pl.BlockSpec(memory_space=pltpu.VMEM)
    RE, CE = R + 2 * W, C + 2 * W
    links = jnp.transpose(pattern, (0, 2, 1))
    operands = (residual, approx_inverse, links, block_aggregate, coarse_inverse)
    return pl.pallas_call(
        functools.partial(kernel, ns, nc, R, C),
        out_shape=pltpu.VMEM(residual.shape, f32),
        in_specs=[pl.BlockSpec(memory_space=pltpu.SMEM)] + [hbm] * 5,
        out_specs=vmem,
        scratch_shapes=[
            pltpu.VMEM(residual.shape, bf16),
            pltpu.VMEM((extent, width, depth), bf16),
            pltpu.SMEM(links.shape, i32),
            pltpu.SMEM(block_aggregate.shape, i32),
            pltpu.VMEM(coarse_inverse.shape, f32),
            pltpu.VMEM((RE, CE, width, sides), bf16),
            pltpu.VMEM((RE, CE, width, sides), bf16),
            pltpu.VMEM((2 * W, CE, width, sides), bf16),
            pltpu.VMEM((R, 2 * W, width, sides), bf16),
            pltpu.VMEM((R, 2 * W, width, sides), bf16),
            pltpu.VMEM((R * C * 4, sides), f32),
            pltpu.VMEM((ns, 4 * owned, sides), f32),
            pltpu.VMEM((ns - 1, 4 * owned, sides), f32),
            pltpu.VMEM((ns * owned, 4, sides), f32),
            dma((5,)),
            dma((4,)), dma((4,)), dma((2,)), dma((2,)), dma((4,)), dma((4,)),
            dma((ns - 1,)), dma((ns - 1,)), dma((ns - 1,)), dma((ns - 1,)),
            dma((4,)), dma((4,)), dma((2,)), dma((2,)), dma((4,)), dma((4,)),
        ],
        compiler_params=pltpu.CompilerParams(
            collective_id=0, has_side_effects=True, vmem_limit_bytes=40 * 1024 * 1024),
        cost_estimate=pl.CostEstimate(
            flops=2 * extent * width * depth * sides,
            bytes_accessed=extent * width * depth * 2 + residual.size * 6,
            transcendentals=0),
    )(live_blocks, *(pltpu.with_memory_space_constraint(array, pltpu.HBM) for array in operands))


def solution(mesh):
    placed = (
        P("stream", "cross", None, None),
        P("stream", "cross", None, None),
        P("stream", "cross", None),
        P("stream", "cross"),
        P("stream", "cross"),
        P("stream", "cross"),
    )
    return jax.shard_map(
        functools.partial(body, mesh.shape["stream"], mesh.shape["cross"]),
        mesh=mesh,
        in_specs=placed,
        out_specs=P("stream", "cross", None, None),
        check_vma=False,
    )
```

```python
import functools

import jax
import jax.numpy as jnp
from jax import lax
from jax.experimental import pallas as pl
from jax.experimental.pallas import tpu as pltpu
from jax.sharding import PartitionSpec as P

W = 2


def kernel(
    ns, nc, R, C,
    live_ref, residual, inverse, pattern_in, aggregate_in, coarse_in,
    out,
    res, a_mat, pattern, aggregate, coarse_inv,
    ext4, fix4, rs, rc, msum, pb, partial, part_in, coarse_all,
    in_sem, h_send, h_recv, t_send, t_recv, q_send, q_recv, p_send, p_recv, g_send, g_recv,
    b_send, b_recv, d_send, d_recv, m_send, m_recv,
):
    s = lax.axis_index("stream")
    c = lax.axis_index("cross")
    width, sides = res.shape[2], res.shape[3]
    CE = C + 2 * W
    RE = R + 2 * W
    owned = coarse_inv.shape[0] // 4
    bf16, f32 = jnp.bfloat16, jnp.float32

    far = lax.rem(s, 2)
    near = 1 - far
    long = lax.rem(c, 2)
    short = 1 - long

    def s_has(d):
        to = s + 2 * d - 1
        return (to >= 0) & (to < ns)

    def c_has(e):
        to = c + 2 * e - 1
        return (to >= 0) & (to < nc)

    def s_to(d):
        return {"stream": jnp.clip(s + 2 * d - 1, 0, ns - 1)}

    def c_to(e):
        return {"cross": jnp.clip(c + 2 * e - 1, 0, nc - 1)}

    loads = [
        pltpu.make_async_copy(residual, res, in_sem.at[0]),
        pltpu.make_async_copy(aggregate_in, aggregate, in_sem.at[1]),
        pltpu.make_async_copy(coarse_in, coarse_inv, in_sem.at[2]),
        pltpu.make_async_copy(pattern_in, pattern, in_sem.at[3]),
        pltpu.make_async_copy(inverse.at[0], a_mat, in_sem.at[4]),
    ]
    loads[0].start()

    barrier = pltpu.get_barrier_semaphore()
    for e in range(2):
        @pl.when(c_has(e))
        def _():
            pl.semaphore_signal(barrier, inc=1, device_id=c_to(e),
                                device_id_type=pl.DeviceIdType.MESH)
    for k in range(1, ns):
        pl.semaphore_signal(barrier, inc=1, device_id={"stream": lax.rem(s + k, ns)},
                            device_id_type=pl.DeviceIdType.MESH)

    for load in loads[1:]:
        load.start()

    def zero(ref, rows, cols):
        ref[rows[0]:rows[1], cols[0]:cols[1]] = jnp.zeros(
            (rows[1] - rows[0], cols[1] - cols[0], width, sides), bf16)

    @pl.when(s == 0)
    def _():
        zero(ext4, (0, W), (0, CE))
        zero(rs, (0, W), (0, CE))

    @pl.when(s == ns - 1)
    def _():
        zero(ext4, (R + W, RE), (0, CE))
        zero(rs, (W, 2 * W), (0, CE))

    @pl.when(c == 0)
    def _():
        zero(ext4, (0, RE), (0, W))
        zero(rc, (0, R), (0, W))

    @pl.when(c == nc - 1)
    def _():
        zero(ext4, (0, RE), (C + W, CE))
        zero(rc, (0, R), (W, 2 * W))

    live = live_ref[0, 0]
    loads[0].wait()

    def mask(cols):
        def row(i, carry):
            for j in cols:
                block = res[i, j]
                keep = jnp.full(block.shape, i * C + j, jnp.int32) < live
                ext4[i + W, j + W] = jnp.where(keep, block.astype(f32), 0.0).astype(bf16)
            return carry

        lax.fori_loop(0, R, row, 0)

    mask(tuple(range(W)) + tuple(range(C - W, C)))

    def own_cols(e):
        return pl.ds(W + e * (C - W), W)

    def halo_cols(e):
        return pl.ds((1 - e) * (C + W), W)

    def side_cols(e):
        return pl.ds(e * (C + W), W)

    mid_cols = pl.ds(W, C)

    def remote(src, dst, send, recv, to):
        return pltpu.make_async_remote_copy(
            src_ref=src, dst_ref=dst, send_sem=send, recv_sem=recv,
            device_id=to, device_id_type=pl.DeviceIdType.MESH)

    def own_rows(d):
        return pl.ds(W + W * d, W)

    def halo_rows(d):
        return pl.ds((1 - d) * (R + W), W)

    def cross1(e, d):
        i = 2 * e + d
        return remote(ext4.at[own_rows(d), own_cols(e)], ext4.at[own_rows(d), halo_cols(e)],
                      h_send.at[i], h_recv.at[i], c_to(e))

    def stream1(d):
        return remote(ext4.at[own_rows(d), mid_cols], ext4.at[halo_rows(d), mid_cols],
                      t_send.at[d], t_recv.at[d], s_to(d))

    def corner1(d, e):
        i = 2 * e + d
        return remote(ext4.at[own_rows(d), side_cols(e)], ext4.at[halo_rows(d), side_cols(e)],
                      q_send.at[i], q_recv.at[i], s_to(d))

    def far_rows(d):
        return pl.ds(d * (R + W), W)

    def corner2(d, e):
        i = 2 * e + d
        return remote(fix4.at[far_rows(d), side_cols(e)], rs.at[pl.ds(W * (1 - d), W), side_cols(e)],
                      b_send.at[i], b_recv.at[i], s_to(d))

    def stream2(d):
        return remote(fix4.at[far_rows(d), mid_cols], rs.at[pl.ds(W * (1 - d), W), mid_cols],
                      d_send.at[d], d_recv.at[d], s_to(d))

    def cross2(e, d):
        i = 2 * e + d
        return remote(msum.at[pl.ds(W * d, W), pl.ds(W * e, W)],
                      rc.at[pl.ds(W * d, W), pl.ds(W * (1 - e), W)],
                      m_send.at[i], m_recv.at[i], c_to(e))

    def when(cond, run):
        pl.when(cond)(run)

    pl.semaphore_wait(barrier, ns - 1 + c_has(0).astype(jnp.int32) + c_has(1).astype(jnp.int32))

    for d in (far, near):
        for e in (long, short):
            when(c_has(e), lambda: cross1(e, d).start())
    mask(range(W, C - W))
    for d in (far, near):
        when(s_has(d), lambda: stream1(d).start())

    def forward(d):
        for e in (short, long):
            @pl.when(c_has(1 - e))
            def _():
                cross1(e, d).wait_recv()
                when(s_has(d), lambda: corner1(d, 1 - e).start())

    forward(far)

    def sums(i, carry):
        for j in range(0, C, 2):
            rows = []
            for u in range(2):
                block = ext4[i + W, j + W + u].astype(f32)
                rows.append(block.reshape(4, width // 4, sides).sum(axis=1))
            first = pl.multiple_of((i * C + j) * 4, 8)
            pb[pl.ds(first, 8), :] = jnp.concatenate(rows, axis=0)
        return carry

    lax.fori_loop(0, R, sums, 0)
    loads[1].wait()
    n_own = R * C
    lane = lax.broadcasted_iota(jnp.int32, (8, 4 * n_own), 1)
    key = jnp.zeros((8, 4 * n_own), jnp.int32)
    for i in range(R):
        for j in range(C):
            key = jnp.where(lane // 4 == i * C + j, aggregate[i, j], key)
    key = (key * 4 + lane % 4)[0:1]
    row = lax.broadcasted_iota(jnp.int32, (4 * owned * ns, 4 * n_own), 0)
    chosen = (row == jnp.broadcast_to(key, row.shape)).astype(f32)
    restricted = jnp.dot(chosen, pb[...], precision=lax.Precision.HIGHEST,
                         preferred_element_type=f32)
    for o in range(ns):
        partial[o] = restricted[o * 4 * owned:(o + 1) * 4 * owned]

    def give(k):
        to = lax.rem(s + k, ns)
        return remote(partial.at[to], part_in.at[k - 1], p_send.at[k - 1], p_recv.at[k - 1],
                      {"stream": to})

    def share(k, mine):
        part = coarse_all.at[pl.ds(mine * owned, owned)]
        return remote(part, part, g_send.at[k - 1], g_recv.at[k - 1],
                      {"stream": lax.rem(s + k, ns)})

    for k in range(1, ns):
        give(k).start()

    forward(near)

    loads[3].wait()
    loads[4].wait()
    for d in range(2):
        when(s_has(1 - d), lambda: stream1(d).wait_recv())
    for d in (near, far):
        for e in range(2):
            when(s_has(1 - d) & c_has(e), lambda: corner1(d, e).wait_recv())

    ext = ext4.reshape(RE * CE, width, sides)

    def fix_of(i, j):
        n = i * CE + j
        picked = jnp.concatenate(
            [ext[pattern[0, k, n]] for k in range(a_mat.shape[2] // width)], axis=0)
        return jnp.dot(a_mat[n], picked, preferred_element_type=f32)

    edge = tuple(range(W)) + tuple(range(C + W, CE))
    middle = tuple(range(W, C + W))

    def put(i, cols):
        for j in cols:
            fix4[i, j] = fix_of(i, j).astype(bf16)

    def fold(d):
        for e in (long, short):
            @pl.when(c_has(e))
            def _():
                when(s_has(d), lambda: corner2(1 - d, e).wait_recv())
                for t in range(W):
                    i = W * d + t
                    for j in range(W):
                        col = e * (C + W) + j
                        msum[i, e * W + j] = (
                            fix4[i + W, col].astype(f32) + rs[i, col].astype(f32)).astype(bf16)
                cross2(e, d).start()

    def coarse_step():
        loads[2].wait()
        total = partial[s]
        for k in range(1, ns):
            give(k).wait_recv()
            total = total + part_in[k - 1]
        coarse = jnp.dot(coarse_inv[...], total, precision=lax.Precision.HIGHEST,
                         preferred_element_type=f32)
        for a in range(owned):
            coarse_all[s * owned + a] = coarse[4 * a:4 * a + 4]
        for k in range(1, ns):
            share(k, s).start()

    def sweep(first, count, cols):
        def row(u, carry):
            put(first + u, cols)
            return carry

        lax.fori_loop(0, count, row, 0)

    def margin(d):
        for u in range(W):
            put(d * (R + W) + u, edge)
        for e in (long, short):
            when(s_has(d) & c_has(e), lambda: corner2(d, e).start())

    def own_edges(d):
        for u in range(W):
            put(W + W * d + u, edge)

    margin(near)
    own_edges(near)
    margin(far)
    fold(near)
    sweep(far * (R + W), W, middle)
    when(s_has(far), lambda: stream2(far).start())
    own_edges(far)
    fold(far)
    coarse_step()
    sweep(near * (R + W), W, middle)
    when(s_has(near), lambda: stream2(near).start())
    sweep(W, R, middle)

    for k in range(1, ns):
        share(k, lax.rem(s + ns - k, ns)).wait_recv()

    def kept(i, j, value):
        keep = jnp.full(value.shape, i * C + j, jnp.int32) < live
        return jnp.where(keep, value, 0.0)

    def finish(d):
        when(s_has(d), lambda: stream2(1 - d).wait_recv())

        def add_stream(u, carry):
            i = W * d + u
            for j in range(C):
                values = coarse_all[aggregate[i, j]]
                spread = jnp.concatenate(
                    [jnp.broadcast_to(values[f:f + 1], (width // 4, sides)) for f in range(4)],
                    axis=0)
                fine = fix4[i + W, j + W].astype(f32) + rs[i, j + W].astype(f32)
                out[i, j] = kept(i, j, fine + spread)
            return carry

        lax.fori_loop(0, W, add_stream, 0)
        for e in (short, long):
            when(c_has(1 - e), lambda: cross2(e, d).wait_recv())
        for u in range(W):
            i = W * d + u
            for j in range(W):
                for col, at in ((j, j), (C - W + j, W + j)):
                    out[i, col] = kept(i, col, out[i, col] + rc[i, at].astype(f32))

    finish(near)
    finish(far)

    for e in range(2):
        @pl.when(c_has(e))
        def _():
            for d in range(2):
                cross1(e, d).wait_send()
                cross2(e, d).wait_send()
    for d in range(2):
        @pl.when(s_has(d))
        def _():
            stream1(d).wait_send()
            stream2(d).wait_send()
            for e in range(2):
                @pl.when(c_has(e))
                def _():
                    corner1(d, e).wait_send()
                    corner2(d, e).wait_send()
    for k in range(1, ns):
        give(k).wait_send()
        share(k, s).wait_send()


def flush(held, out, sem):
    half = held.shape[1] // 2
    copies = [
        pltpu.make_async_copy(held.at[i, pl.ds(h * half, half)], out.at[i, pl.ds(h * half, half)],
                              sem.at[2 * i + h])
        for i in range(held.shape[0]) for h in range(2)]
    for copy in copies:
        copy.start()
    for copy in copies:
        copy.wait()


def body(ns, nc, residual, approx_inverse, pattern, live_blocks, block_aggregate, coarse_inverse):
    R, C, width, sides = residual.shape
    _, extent, _, depth = approx_inverse.shape
    owned = coarse_inverse.shape[0] // 4
    bf16, f32, i32 = jnp.bfloat16, jnp.float32, jnp.int32
    dma = pltpu.SemaphoreType.DMA
    hbm = pl.BlockSpec(memory_space=pltpu.HBM)
    vmem = pl.BlockSpec(memory_space=pltpu.VMEM)
    RE, CE = R + 2 * W, C + 2 * W
    links = jnp.transpose(pattern, (0, 2, 1))
    operands = (residual, approx_inverse, links, block_aggregate, coarse_inverse)
    held = pl.pallas_call(
        functools.partial(kernel, ns, nc, R, C),
        out_shape=pltpu.VMEM(residual.shape, f32),
        in_specs=[pl.BlockSpec(memory_space=pltpu.SMEM)] + [hbm] * 5,
        out_specs=vmem,
        scratch_shapes=[
            pltpu.VMEM(residual.shape, bf16),
            pltpu.VMEM((extent, width, depth), bf16),
            pltpu.SMEM(links.shape, i32),
            pltpu.SMEM(block_aggregate.shape, i32),
            pltpu.VMEM(coarse_inverse.shape, f32),
            pltpu.VMEM((RE, CE, width, sides), bf16),
            pltpu.VMEM((RE, CE, width, sides), bf16),
            pltpu.VMEM((2 * W, CE, width, sides), bf16),
            pltpu.VMEM((R, 2 * W, width, sides), bf16),
            pltpu.VMEM((R, 2 * W, width, sides), bf16),
            pltpu.VMEM((R * C * 4, sides), f32),
            pltpu.VMEM((ns, 4 * owned, sides), f32),
            pltpu.VMEM((ns - 1, 4 * owned, sides), f32),
            pltpu.VMEM((ns * owned, 4, sides), f32),
            dma((5,)),
            dma((4,)), dma((4,)), dma((2,)), dma((2,)), dma((4,)), dma((4,)),
            dma((ns - 1,)), dma((ns - 1,)), dma((ns - 1,)), dma((ns - 1,)),
            dma((4,)), dma((4,)), dma((2,)), dma((2,)), dma((4,)), dma((4,)),
        ],
        compiler_params=pltpu.CompilerParams(
            collective_id=0, has_side_effects=True, vmem_limit_bytes=40 * 1024 * 1024),
        cost_estimate=pl.CostEstimate(
            flops=2 * extent * width * depth * sides,
            bytes_accessed=extent * width * depth * 2 + residual.size * 6,
            transcendentals=0),
    )(live_blocks, *(pltpu.with_memory_space_constraint(array, pltpu.HBM) for array in operands))
    return pl.pallas_call(
        flush,
        out_shape=jax.ShapeDtypeStruct(residual.shape, f32),
        in_specs=[vmem],
        out_specs=hbm,
        scratch_shapes=[dma((2 * R,))],
        cost_estimate=pl.CostEstimate(flops=0, bytes_accessed=residual.size * 4, transcendentals=0),
    )(held)


def solution(mesh):
    placed = (
        P("stream", "cross", None, None),
        P("stream", "cross", None, None),
        P("stream", "cross", None),
        P("stream", "cross"),
        P("stream", "cross"),
        P("stream", "cross"),
    )
    return jax.shard_map(
        functools.partial(body, mesh.shape["stream"], mesh.shape["cross"]),
        mesh=mesh,
        in_specs=placed,
        out_specs=P("stream", "cross", None, None),
        check_vma=False,
    )
```

```python
import functools

import jax
import jax.numpy as jnp
from jax import lax
from jax.experimental import pallas as pl
from jax.experimental.pallas import tpu as pltpu
from jax.sharding import PartitionSpec as P

W = 2


def kernel(
    ns, nc, R, C,
    live_ref, residual, inverse, pattern_in, aggregate_in, coarse_in,
    out,
    res, a_mat, pattern, aggregate, coarse_inv,
    ext4, fix4, rs, rc, msum, pb, partial, part_in, coarse_all,
    in_sem, h_send, h_recv, t_send, t_recv, q_send, q_recv, p_send, p_recv, g_send, g_recv,
    b_send, b_recv, d_send, d_recv, m_send, m_recv,
):
    s = lax.axis_index("stream")
    c = lax.axis_index("cross")
    width, sides = res.shape[2], res.shape[3]
    CE = C + 2 * W
    RE = R + 2 * W
    owned = coarse_inv.shape[0] // 4
    bf16, f32 = jnp.bfloat16, jnp.float32

    far = lax.rem(s, 2)
    near = 1 - far
    long = lax.rem(c, 2)
    short = 1 - long

    def s_has(d):
        to = s + 2 * d - 1
        return (to >= 0) & (to < ns)

    def c_has(e):
        to = c + 2 * e - 1
        return (to >= 0) & (to < nc)

    def s_to(d):
        return {"stream": jnp.clip(s + 2 * d - 1, 0, ns - 1)}

    def c_to(e):
        return {"cross": jnp.clip(c + 2 * e - 1, 0, nc - 1)}

    parts = (pl.ds(0, W), pl.ds(C - W, W), pl.ds(W, C - 2 * W))
    first = [
        pltpu.make_async_copy(residual.at[:, part], res.at[:, part], in_sem.at[5 + n])
        for n, part in enumerate(parts)]
    loads = [
        None,
        pltpu.make_async_copy(aggregate_in, aggregate, in_sem.at[1]),
        pltpu.make_async_copy(coarse_in, coarse_inv, in_sem.at[2]),
        pltpu.make_async_copy(pattern_in, pattern, in_sem.at[3]),
        pltpu.make_async_copy(inverse.at[0], a_mat, in_sem.at[4]),
    ]
    for load in first:
        load.start()

    barrier = pltpu.get_barrier_semaphore()
    for e in range(2):
        @pl.when(c_has(e))
        def _():
            pl.semaphore_signal(barrier, inc=1, device_id=c_to(e),
                                device_id_type=pl.DeviceIdType.MESH)
    for k in range(1, ns):
        pl.semaphore_signal(barrier, inc=1, device_id={"stream": lax.rem(s + k, ns)},
                            device_id_type=pl.DeviceIdType.MESH)

    for load in loads[1:]:
        load.start()

    def zero(ref, rows, cols):
        ref[rows[0]:rows[1], cols[0]:cols[1]] = jnp.zeros(
            (rows[1] - rows[0], cols[1] - cols[0], width, sides), bf16)

    @pl.when(s == 0)
    def _():
        zero(ext4, (0, W), (0, CE))
        zero(rs, (0, W), (0, CE))

    @pl.when(s == ns - 1)
    def _():
        zero(ext4, (R + W, RE), (0, CE))
        zero(rs, (W, 2 * W), (0, CE))

    @pl.when(c == 0)
    def _():
        zero(ext4, (0, RE), (0, W))
        zero(rc, (0, R), (0, W))

    @pl.when(c == nc - 1)
    def _():
        zero(ext4, (0, RE), (C + W, CE))
        zero(rc, (0, R), (W, 2 * W))

    live = live_ref[0, 0]
    first[0].wait()
    first[1].wait()

    def mask(cols):
        def row(i, carry):
            for j in cols:
                block = res[i, j]
                keep = jnp.full(block.shape, i * C + j, jnp.int32) < live
                ext4[i + W, j + W] = jnp.where(keep, block.astype(f32), 0.0).astype(bf16)
            return carry

        lax.fori_loop(0, R, row, 0)

    mask(tuple(range(W)) + tuple(range(C - W, C)))

    def own_cols(e):
        return pl.ds(W + e * (C - W), W)

    def halo_cols(e):
        return pl.ds((1 - e) * (C + W), W)

    def side_cols(e):
        return pl.ds(e * (C + W), W)

    mid_cols = pl.ds(W, C)

    def remote(src, dst, send, recv, to):
        return pltpu.make_async_remote_copy(
            src_ref=src, dst_ref=dst, send_sem=send, recv_sem=recv,
            device_id=to, device_id_type=pl.DeviceIdType.MESH)

    def own_rows(d):
        return pl.ds(W + W * d, W)

    def halo_rows(d):
        return pl.ds((1 - d) * (R + W), W)

    def cross1(e, d):
        i = 2 * e + d
        return remote(ext4.at[own_rows(d), own_cols(e)], ext4.at[own_rows(d), halo_cols(e)],
                      h_send.at[i], h_recv.at[i], c_to(e))

    def stream1(d):
        return remote(ext4.at[own_rows(d), mid_cols], ext4.at[halo_rows(d), mid_cols],
                      t_send.at[d], t_recv.at[d], s_to(d))

    def corner1(d, e):
        i = 2 * e + d
        return remote(ext4.at[own_rows(d), side_cols(e)], ext4.at[halo_rows(d), side_cols(e)],
                      q_send.at[i], q_recv.at[i], s_to(d))

    def far_rows(d):
        return pl.ds(d * (R + W), W)

    def corner2(d, e):
        i = 2 * e + d
        return remote(fix4.at[far_rows(d), side_cols(e)], rs.at[pl.ds(W * (1 - d), W), side_cols(e)],
                      b_send.at[i], b_recv.at[i], s_to(d))

    def stream2(d):
        return remote(fix4.at[far_rows(d), mid_cols], rs.at[pl.ds(W * (1 - d), W), mid_cols],
                      d_send.at[d], d_recv.at[d], s_to(d))

    def cross2(e, d):
        i = 2 * e + d
        return remote(msum.at[pl.ds(W * d, W), pl.ds(W * e, W)],
                      rc.at[pl.ds(W * d, W), pl.ds(W * (1 - e), W)],
                      m_send.at[i], m_recv.at[i], c_to(e))

    def when(cond, run):
        pl.when(cond)(run)

    pl.semaphore_wait(barrier, ns - 1 + c_has(0).astype(jnp.int32) + c_has(1).astype(jnp.int32))

    for d in (far, near):
        for e in (long, short):
            when(c_has(e), lambda: cross1(e, d).start())
    first[2].wait()
    mask(range(W, C - W))
    for d in (far, near):
        when(s_has(d), lambda: stream1(d).start())

    def forward(d):
        for e in (short, long):
            @pl.when(c_has(1 - e))
            def _():
                cross1(e, d).wait_recv()
                when(s_has(d), lambda: corner1(d, 1 - e).start())

    forward(far)

    def sums(i, carry):
        for j in range(0, C, 2):
            rows = []
            for u in range(2):
                block = ext4[i + W, j + W + u].astype(f32)
                rows.append(block.reshape(4, width // 4, sides).sum(axis=1))
            first = pl.multiple_of((i * C + j) * 4, 8)
            pb[pl.ds(first, 8), :] = jnp.concatenate(rows, axis=0)
        return carry

    lax.fori_loop(0, R, sums, 0)
    loads[1].wait()
    n_own = R * C
    lane = lax.broadcasted_iota(jnp.int32, (8, 4 * n_own), 1)
    key = jnp.zeros((8, 4 * n_own), jnp.int32)
    for i in range(R):
        for j in range(C):
            key = jnp.where(lane // 4 == i * C + j, aggregate[i, j], key)
    key = (key * 4 + lane % 4)[0:1]
    row = lax.broadcasted_iota(jnp.int32, (4 * owned * ns, 4 * n_own), 0)
    chosen = (row == jnp.broadcast_to(key, row.shape)).astype(f32)
    restricted = jnp.dot(chosen, pb[...], precision=lax.Precision.HIGHEST,
                         preferred_element_type=f32)
    for o in range(ns):
        partial[o] = restricted[o * 4 * owned:(o + 1) * 4 * owned]

    def give(k):
        to = lax.rem(s + k, ns)
        return remote(partial.at[to], part_in.at[k - 1], p_send.at[k - 1], p_recv.at[k - 1],
                      {"stream": to})

    def share(k, mine):
        part = coarse_all.at[pl.ds(mine * owned, owned)]
        return remote(part, part, g_send.at[k - 1], g_recv.at[k - 1],
                      {"stream": lax.rem(s + k, ns)})

    for k in range(1, ns):
        give(k).start()

    forward(near)

    loads[3].wait()
    loads[4].wait()
    for d in range(2):
        when(s_has(1 - d), lambda: stream1(d).wait_recv())
    for d in (near, far):
        for e in range(2):
            when(s_has(1 - d) & c_has(e), lambda: corner1(d, e).wait_recv())

    ext = ext4.reshape(RE * CE, width, sides)

    def fix_of(i, j):
        n = i * CE + j
        picked = jnp.concatenate(
            [ext[pattern[0, k, n]] for k in range(a_mat.shape[2] // width)], axis=0)
        return jnp.dot(a_mat[n], picked, preferred_element_type=f32)

    edge = tuple(range(W)) + tuple(range(C + W, CE))
    middle = tuple(range(W, C + W))

    def put(i, cols):
        for j in cols:
            fix4[i, j] = fix_of(i, j).astype(bf16)

    def fold(d):
        for e in (long, short):
            @pl.when(c_has(e))
            def _():
                when(s_has(d), lambda: corner2(1 - d, e).wait_recv())
                for t in range(W):
                    i = W * d + t
                    for j in range(W):
                        col = e * (C + W) + j
                        msum[i, e * W + j] = (
                            fix4[i + W, col].astype(f32) + rs[i, col].astype(f32)).astype(bf16)
                cross2(e, d).start()

    def coarse_step():
        loads[2].wait()
        total = partial[s]
        for k in range(1, ns):
            give(k).wait_recv()
            total = total + part_in[k - 1]
        coarse = jnp.dot(coarse_inv[...], total, precision=lax.Precision.HIGHEST,
                         preferred_element_type=f32)
        for a in range(owned):
            coarse_all[s * owned + a] = coarse[4 * a:4 * a + 4]
        for k in range(1, ns):
            share(k, s).start()

    def sweep(first, count, cols):
        def row(u, carry):
            put(first + u, cols)
            return carry

        lax.fori_loop(0, count, row, 0)

    def margin(d):
        for u in range(W):
            put(d * (R + W) + u, edge)
        for e in (long, short):
            when(s_has(d) & c_has(e), lambda: corner2(d, e).start())

    def own_edges(d):
        for u in range(W):
            put(W + W * d + u, edge)

    margin(near)
    own_edges(near)
    margin(far)
    fold(near)
    sweep(far * (R + W), W, middle)
    when(s_has(far), lambda: stream2(far).start())
    own_edges(far)
    fold(far)
    coarse_step()
    sweep(near * (R + W), W, middle)
    when(s_has(near), lambda: stream2(near).start())
    sweep(W, R, middle)

    for k in range(1, ns):
        share(k, lax.rem(s + ns - k, ns)).wait_recv()

    def kept(i, j, value):
        keep = jnp.full(value.shape, i * C + j, jnp.int32) < live
        return jnp.where(keep, value, 0.0)

    def finish(d):
        when(s_has(d), lambda: stream2(1 - d).wait_recv())

        def add_stream(u, carry):
            i = W * d + u
            for j in range(C):
                values = coarse_all[aggregate[i, j]]
                spread = jnp.concatenate(
                    [jnp.broadcast_to(values[f:f + 1], (width // 4, sides)) for f in range(4)],
                    axis=0)
                fine = fix4[i + W, j + W].astype(f32) + rs[i, j + W].astype(f32)
                out[i, j] = kept(i, j, fine + spread)
            return carry

        lax.fori_loop(0, W, add_stream, 0)
        for e in (short, long):
            when(c_has(1 - e), lambda: cross2(e, d).wait_recv())
        for u in range(W):
            i = W * d + u
            for j in range(W):
                for col, at in ((j, j), (C - W + j, W + j)):
                    out[i, col] = kept(i, col, out[i, col] + rc[i, at].astype(f32))

    finish(near)
    finish(far)

    for e in range(2):
        @pl.when(c_has(e))
        def _():
            for d in range(2):
                cross1(e, d).wait_send()
                cross2(e, d).wait_send()
    for d in range(2):
        @pl.when(s_has(d))
        def _():
            stream1(d).wait_send()
            stream2(d).wait_send()
            for e in range(2):
                @pl.when(c_has(e))
                def _():
                    corner1(d, e).wait_send()
                    corner2(d, e).wait_send()
    for k in range(1, ns):
        give(k).wait_send()
        share(k, s).wait_send()


def body(ns, nc, residual, approx_inverse, pattern, live_blocks, block_aggregate, coarse_inverse):
    R, C, width, sides = residual.shape
    _, extent, _, depth = approx_inverse.shape
    owned = coarse_inverse.shape[0] // 4
    bf16, f32, i32 = jnp.bfloat16, jnp.float32, jnp.int32
    dma = pltpu.SemaphoreType.DMA
    hbm = pl.BlockSpec(memory_space=pltpu.HBM)
    vmem = pl.BlockSpec(memory_space=pltpu.VMEM)
    RE, CE = R + 2 * W, C + 2 * W
    links = jnp.transpose(pattern, (0, 2, 1))
    operands = (residual, approx_inverse, links, block_aggregate, coarse_inverse)
    return pl.pallas_call(
        functools.partial(kernel, ns, nc, R, C),
        out_shape=pltpu.VMEM(residual.shape, f32),
        in_specs=[pl.BlockSpec(memory_space=pltpu.SMEM)] + [hbm] * 5,
        out_specs=vmem,
        scratch_shapes=[
            pltpu.VMEM(residual.shape, bf16),
            pltpu.VMEM((extent, width, depth), bf16),
            pltpu.SMEM(links.shape, i32),
            pltpu.SMEM(block_aggregate.shape, i32),
            pltpu.VMEM(coarse_inverse.shape, f32),
            pltpu.VMEM((RE, CE, width, sides), bf16),
            pltpu.VMEM((RE, CE, width, sides), bf16),
            pltpu.VMEM((2 * W, CE, width, sides), bf16),
            pltpu.VMEM((R, 2 * W, width, sides), bf16),
            pltpu.VMEM((R, 2 * W, width, sides), bf16),
            pltpu.VMEM((R * C * 4, sides), f32),
            pltpu.VMEM((ns, 4 * owned, sides), f32),
            pltpu.VMEM((ns - 1, 4 * owned, sides), f32),
            pltpu.VMEM((ns * owned, 4, sides), f32),
            dma((8,)),
            dma((4,)), dma((4,)), dma((2,)), dma((2,)), dma((4,)), dma((4,)),
            dma((ns - 1,)), dma((ns - 1,)), dma((ns - 1,)), dma((ns - 1,)),
            dma((4,)), dma((4,)), dma((2,)), dma((2,)), dma((4,)), dma((4,)),
        ],
        compiler_params=pltpu.CompilerParams(
            collective_id=0, has_side_effects=True, vmem_limit_bytes=40 * 1024 * 1024),
        cost_estimate=pl.CostEstimate(
            flops=2 * extent * width * depth * sides,
            bytes_accessed=extent * width * depth * 2 + residual.size * 6,
            transcendentals=0),
    )(live_blocks, *(pltpu.with_memory_space_constraint(array, pltpu.HBM) for array in operands))


def solution(mesh):
    placed = (
        P("stream", "cross", None, None),
        P("stream", "cross", None, None),
        P("stream", "cross", None),
        P("stream", "cross"),
        P("stream", "cross"),
        P("stream", "cross"),
    )
    return jax.shard_map(
        functools.partial(body, mesh.shape["stream"], mesh.shape["cross"]),
        mesh=mesh,
        in_specs=placed,
        out_specs=P("stream", "cross", None, None),
        check_vma=False,
    )
```
